32 devices in a mesh: groups: 2 (over y), tile: 4 (over z), sect: 2 (over x), chan: 2 (over core).
Axes of the slice: x: 2, y: 2, z: 4, core: 2. Of those that a mesh axis runs over, the one named last changes fastest.
Arguments:
- fine: bfloat16 [4, 2, 192, 64, 256], P(('groups', 'chan'), 'sect', 'tile'), parts along dimension 0, may hold values from -6 to 6
- conv_spatial: bfloat16 [4, 256, 256], replicated, may hold values from -0.375 to 0.375
- conv_mix: bfloat16 [5, 64, 64], replicated, may hold values from -0.3125 to 0.3125
- neighbours: int32 [2, 192, 5], P('sect', 'tile'), may hold values from 0 to 191, as said below
- fine_codes: int32 [2, 192, 5], P('sect', 'tile'), may hold values from 0 to 3
- restrict: bfloat16 [4, 256, 16], replicated, may hold values from -0.375 to 0.375
- restrict_codes: int32 [2, 192], P('sect', 'tile'), may hold values from 0 to 3
- route: int32 [2, 192], P('sect'), may hold values from 0 to 191, as said below
- coarse_spatial: bfloat16 [4, 256, 256], replicated, may hold values from -0.375 to 0.375
- coarse_mix: bfloat16 [4, 64, 64], replicated, may hold values from -0.375 to 0.375
- coarse_codes: int32 [2, 12, 3], P('sect', 'tile'), may hold values from 0 to 3
Outputs:
- fine_skip: bfloat16 [4, 2, 192, 64, 256], P(('groups', 'chan'), 'sect', 'tile'), parts along dimension 0
- coarse_out: bfloat16 [4, 2, 12, 64, 256], P(('groups', 'chan'), 'sect', 'tile'), parts along dimension 0
The draws below stay inside these ranges and needn't reach their ends.
There are 2 independent parts, one for each index of `groups`. The reference program is written for one: setup_inputs(seed, part) draws one part's arguments, and reference() takes and returns one part's arrays. A program takes and returns all parts, laid end to end along the dimension named above; an argument that names none is the same for every part. Nothing has to cross between parts.
Inputs may be any that keep to these rules, and one draw needn't show every extreme that they name: (neighbours[s, b, t] - b) modulo 192 lies within -2 .. 2. `route`: each row is a permutation of the coarse slots; the fine blocks of each aligned run of 48 (one tile device) go exactly 12 to the slots of each aligned block of 48 slots.
All inputs are finite; a program needn't handle non-finite values.
Results may differ from the reference program's by a relative error of at most 0.0062.
Values may be sent and summed in bfloat16 or wider, within the bound.
No kernel may reach another device: no remote copies, remote signals or barrier semaphores. Data moves between devices by JAX's collectives and lax.ppermute only.
A program may use at most 128 MiB of HBM per device.

```python
import jax
import jax.numpy as jnp
from jax import lax

CH = 64
FB = 256
CQ = 16
PIECES = 16
TAPS = 5
ROTATIONS = 4
RIM = 2
FBD = 48
BATCH = 2
SECTS = 2
NTB = 192
NCB = 12
COARSE_CELLS = 256


def draw_neighbours(key, part):
    offsets = jax.random.randint(jax.random.fold_in(key, 11), (SECTS, NTB, TAPS), -RIM, RIM + 1)
    blocks = jnp.arange(NTB, dtype=jnp.int32)[None, :, None]
    return ((blocks + offsets) % NTB).astype(jnp.int32)


def draw_route(key, part):
    tiles = NTB // FBD
    per_peer = FBD // tiles
    first_key = jax.random.fold_in(key, 21)
    second_key = jax.random.fold_in(key, 22)
    slot_perms = jax.vmap(lambda inner: jax.random.permutation(inner, FBD))(jax.random.split(first_key, SECTS * tiles))
    slot_perms = slot_perms.reshape(SECTS, tiles, FBD)
    source = jnp.arange(tiles, dtype=jnp.int32)[:, None]
    within = jnp.arange(FBD, dtype=jnp.int32)[None, :]
    target = jnp.broadcast_to(within % tiles, (tiles, FBD))
    rank = source * per_peer + within // tiles
    position = slot_perms[:, target, rank]
    slots = target[None] * FBD + position
    shuffles = jax.vmap(lambda inner: jax.random.permutation(inner, FBD))(jax.random.split(second_key, SECTS * tiles))
    shuffles = shuffles.reshape(SECTS, tiles, FBD)
    mixed_slots = jnp.take_along_axis(slots, shuffles, axis=2)
    return mixed_slots.reshape(SECTS, NTB).astype(jnp.int32)


def plant(drawn, own_key, low, high):
    dims = drawn.shape
    spot = [jax.random.randint(jax.random.fold_in(own_key, axis), (), 0, dims[axis]) for axis in range(len(dims))]
    drawn = drawn.at[tuple(spot)].set(low)
    longest = dims.index(max(dims))
    spot[longest] = (spot[longest] + 1) % dims[longest]
    return drawn.at[tuple(spot)].set(high)


def levels(own_key, shape, cuts, least, high):
    loudness = 1.0
    for axis_at, blocks in cuts:
        heights = jax.random.uniform(jax.random.fold_in(jax.random.fold_in(own_key, 6), axis_at), (blocks,), jnp.float32, least / len(cuts), high / len(cuts))
        loudness = loudness * jnp.repeat(jnp.exp(heights), shape[axis_at] // blocks).reshape((-1,) + (1,) * (len(shape) - 1 - axis_at))
    return loudness


def bell_draw(own_key, dims, deviation, most, cuts=(), kind=jnp.bfloat16):
    result = deviation * jax.random.normal(own_key, dims, jnp.float32)
    if cuts:
        result = result * levels(own_key, dims, cuts, -0.22, 0.18)
    return jnp.clip(result, -most, most).astype(kind)


def setup_inputs(seed: int = 0, part: int = 0) -> dict:
    key_of = jax.random.split(jax.random.key(seed), 12)
    own_keys = jax.random.split(jax.random.fold_in(key_of[11], part), 12)
    fine = bell_draw(own_keys[0], (BATCH, SECTS, NTB, CH, FB), 1.0, 6.0, ((0, 2), (1, 2), (2, 4)))
    conv_spatial = bell_draw(key_of[1], (ROTATIONS, FB, FB), FB ** -0.5, 0.375)
    conv_mix = bell_draw(key_of[2], (TAPS, CH, CH), (TAPS * CH) ** -0.5, 0.3125)
    neighbours = draw_neighbours(jax.random.fold_in(key_of[11], 71), part)
    fine_codes = plant(jax.random.randint(key_of[4], (SECTS, NTB, TAPS), 0, ROTATIONS), jax.random.fold_in(key_of[4], 1), 0, ROTATIONS - 1).astype(jnp.int32)
    restrict = bell_draw(key_of[5], (ROTATIONS, FB, CQ), FB ** -0.5, 0.375)
    restrict_codes = plant(jax.random.randint(key_of[6], (SECTS, NTB), 0, ROTATIONS), jax.random.fold_in(key_of[6], 1), 0, ROTATIONS - 1).astype(jnp.int32)
    route = draw_route(jax.random.fold_in(key_of[11], 71), part)
    coarse_spatial = bell_draw(key_of[8], (ROTATIONS, COARSE_CELLS, COARSE_CELLS), COARSE_CELLS ** -0.5, 0.375)
    coarse_mix = bell_draw(key_of[9], (4, CH, CH), (4 * CH) ** -0.5, 0.375)
    coarse_codes = plant(jax.random.randint(key_of[10], (SECTS, NCB, 3), 0, ROTATIONS), jax.random.fold_in(key_of[10], 1), 0, ROTATIONS - 1).astype(jnp.int32)
    return dict(fine=fine, conv_spatial=conv_spatial, conv_mix=conv_mix, neighbours=neighbours, fine_codes=fine_codes, restrict=restrict, restrict_codes=restrict_codes, route=route, coarse_spatial=coarse_spatial, coarse_mix=coarse_mix, coarse_codes=coarse_codes)


def fine_section(operands):
    block_rows, neighbours, fine_codes, restrict_codes, route, conv_spatial, conv_mix, restrict = operands
    mixed = jnp.zeros(block_rows.shape, jnp.float32)
    for term_index in range(TAPS):
        rows = jnp.take(block_rows, neighbours[:, term_index], axis=0).astype(jnp.float32)
        spatial = jnp.take(conv_spatial, fine_codes[:, term_index], axis=0).astype(jnp.float32)
        term = jnp.einsum("bcf,bfg->bcg", rows, spatial).astype(jnp.bfloat16)
        mixed = mixed + jnp.einsum("dc,bcg->bdg", conv_mix[term_index].astype(jnp.float32), term.astype(jnp.float32))
    fine_skip = (block_rows.astype(jnp.float32) + jax.nn.silu(mixed)).astype(jnp.bfloat16)
    chosen = jnp.take(restrict, restrict_codes, axis=0).astype(jnp.float32)
    piece = jnp.einsum("bcf,bfq->bcq", fine_skip.astype(jnp.float32), chosen).astype(jnp.bfloat16)
    placed = jnp.zeros(piece.shape, jnp.bfloat16).at[route].set(piece)
    coarse = placed.reshape(NCB, PIECES, CH, CQ).transpose(0, 2, 1, 3).reshape(NCB, CH, COARSE_CELLS)
    return fine_skip, coarse


def reference(fine, conv_spatial, conv_mix, neighbours, fine_codes, restrict, restrict_codes, route, coarse_spatial, coarse_mix, coarse_codes):
    flat_fine = fine.reshape(BATCH * SECTS, NTB, CH, FB)
    tiled_nb = jnp.tile(neighbours, (BATCH, 1, 1))
    tiled_fc = jnp.tile(fine_codes, (BATCH, 1, 1))
    tiled_rc = jnp.tile(restrict_codes, (BATCH, 1))
    tiled_rt = jnp.tile(route, (BATCH, 1))

    def one_section(operands):
        return fine_section(operands + (conv_spatial, conv_mix, restrict))

    fine_skip, coarse = lax.map(one_section, (flat_fine, tiled_nb, tiled_fc, tiled_rc, tiled_rt))
    fine_skip = fine_skip.reshape(BATCH, SECTS, NTB, CH, FB)
    coarse = coarse.reshape(BATCH, SECTS, NCB, CH, COARSE_CELLS)
    left = jnp.roll(coarse, 1, axis=2)
    right = jnp.roll(coarse, -1, axis=2)
    seam = jnp.roll(coarse, 1, axis=1)
    total = jnp.einsum("dc,bsncg->bsndg", coarse_mix[0].astype(jnp.float32), coarse.astype(jnp.float32))
    for edge_index, beside in enumerate([left, right, seam]):
        spatial = jnp.take(coarse_spatial, coarse_codes[:, :, edge_index], axis=0).astype(jnp.float32)
        edge = jnp.einsum("bsncg,snge->bsnce", beside.astype(jnp.float32), spatial).astype(jnp.bfloat16)
        total = total + jnp.einsum("dc,bsnce->bsnde", coarse_mix[edge_index + 1].astype(jnp.float32), edge.astype(jnp.float32))
    coarse_out = (coarse.astype(jnp.float32) + jax.nn.silu(total)).astype(jnp.bfloat16)
    return fine_skip, coarse_out
```

```python
import functools

import jax
import jax.numpy as jnp
from jax import lax
from jax.experimental import pallas as pl
from jax.experimental.pallas import tpu as pltpu
from jax.sharding import PartitionSpec as P

LANES = 128
RIM = 2
EDGE = 2 * RIM
CHUNK = 8
VMEM_BYTES = 48 * 1024 * 1024

SMEM = functools.partial(pl.BlockSpec, memory_space=pltpu.SMEM)
VMEM = functools.partial(pl.BlockSpec, memory_space=pltpu.VMEM)
ANY = functools.partial(pl.BlockSpec, memory_space=pl.ANY)
F32 = jnp.float32
BF16 = jnp.bfloat16


def dot(a, b):
    return jnp.dot(a, b, preferred_element_type=F32)


def silu(v):
    return v * (0.5 + 0.5 * jnp.tanh(0.5 * v))


def shifted(value, axis, steps):
    count = lax.axis_size(axis)
    return lax.ppermute(value, axis, [(i, (i + steps) % count) for i in range(count)])


def rotations_of(table_ref, rows, store):
    for rotation in range(table_ref.shape[0]):
        store(rotation, dot(rows, table_ref[rotation]).astype(BF16))


def joined_mix(mix_ref, terms):
    return jnp.concatenate([mix_ref[t] for t in range(terms)], axis=1)


def stacked_restrict(restrict_ref):
    parts = [restrict_ref[r].astype(F32) for r in range(restrict_ref.shape[0])]
    width = sum(p.shape[1] for p in parts)
    return jnp.concatenate(parts * (LANES // width), axis=1).astype(BF16)


def mixed_skip(y_ref, y_index, taps, mix_wide, mix_ref, own):
    terms = [y_ref[y_index(t)] for t in range(taps)]
    wide = mix_wide.shape[1] // mix_ref.shape[1]
    mixed = dot(mix_wide, jnp.concatenate(terms[:wide], axis=0))
    for t in range(wide, taps):
        mixed = mixed + dot(mix_ref[t], terms[t])
    return (own.astype(F32) + silu(mixed)).astype(BF16)


def place(acc_ref, at, product, code, rank, cq):
    per = LANES // cq
    slot = lax.rem(rank, per)
    amount = lax.rem((slot - code) * cq + LANES, LANES)
    turned = pltpu.roll(product, amount, axis=1)
    lane = lax.broadcasted_iota(jnp.int32, turned.shape, 1)
    at = at + lax.div(rank, per)
    acc_ref[at] = jnp.where(lax.div(lane, cq) == slot, turned, acc_ref[at])


def next_rank(counts_ref, dest):
    rank = counts_ref[dest]
    counts_ref[dest] = rank + 1
    return rank


def inner_kernel(
    nbr_ref, code_ref, rcode_ref, route_ref, x_ref, spatial_ref, mix_ref, restrict_ref,
    skip_ref, acc_ref, y_ref, counts_ref,
):
    count = x_ref.shape[0]
    channels, cells = x_ref.shape[1:]
    cq = restrict_ref.shape[2]
    taps = mix_ref.shape[0]
    tiles = route_ref.shape[1] // count
    halves = acc_ref.shape[0] // tiles
    me = lax.axis_index("tile")

    @pl.loop(0, count // CHUNK)
    def _(step):
        base = step * CHUNK
        rows = x_ref[pl.ds(base, CHUNK)].reshape(CHUNK * channels, cells)

        def store(rotation, value):
            y_ref[pl.ds(rotation * count + base, CHUNK)] = value.reshape(CHUNK, channels, cells)

        rotations_of(spatial_ref, rows, store)

    for d in range(tiles):
        counts_ref[d] = 0
    mix_wide = joined_mix(mix_ref, min(taps, cells // channels))
    stacked = stacked_restrict(restrict_ref)

    @pl.loop(0, count // CHUNK)
    def _(step):
        base = step * CHUNK
        for i in range(CHUNK):
            b = base + i

            def y_index(t):
                local = nbr_ref[b, t] - me * count
                local = jnp.clip(local, 0, count - 1)
                return code_ref[b, t] * count + local

            skip_ref[b] = mixed_skip(y_ref, y_index, taps, mix_wide, mix_ref, x_ref[b])
        rows = skip_ref[pl.ds(base, CHUNK)].reshape(CHUNK * channels, cells)
        products = dot(rows, stacked)
        for i in range(CHUNK):
            b = base + i
            dest = lax.div(route_ref[0, me * count + b], count)
            rank = next_rank(counts_ref, dest)
            hop = lax.rem(dest - me + tiles, tiles)
            place(
                acc_ref, hop * halves, products[i * channels:(i + 1) * channels],
                rcode_ref[0, b], rank, cq,
            )


def rim_kernel(
    nbr_ref, code_ref, rcode_ref, route_ref, before_ref, head_ref, tail_ref, after_ref,
    spatial_ref, mix_ref, restrict_ref, acc_in_ref, skip_in_ref,
    skip_ref, *refs,
):
    out_refs, (acc_ref, x_ref, y_ref, done_ref, counts_ref, sem) = refs[:-6], refs[-6:]
    del skip_in_ref
    count = rcode_ref.shape[1]
    channels, cells = head_ref.shape[1:]
    cq = restrict_ref.shape[2]
    taps = mix_ref.shape[0]
    blocks = route_ref.shape[1]
    tiles = blocks // count
    halves = acc_ref.shape[0] // tiles
    me = lax.axis_index("tile")
    side = EDGE + RIM

    x_ref[0:RIM] = before_ref[...]
    x_ref[RIM:side] = head_ref[...]
    x_ref[side:side + EDGE] = tail_ref[...]
    x_ref[side + EDGE:] = after_ref[...]
    rows = x_ref[...].reshape(2 * side * channels, cells)

    def store(rotation, value):
        y_ref[rotation * 2 * side:(rotation + 1) * 2 * side] = value.reshape(2 * side, channels, cells)

    rotations_of(spatial_ref, rows, store)
    acc_ref[...] = acc_in_ref[...]
    mix_wide = joined_mix(mix_ref, min(taps, cells // channels))
    stacked = stacked_restrict(restrict_ref)
    outer = [b for b in range(RIM)] + [count - RIM + b for b in range(RIM)]
    for i, b in enumerate(outer):
        first = 0 if i < RIM else count + 2 * RIM - side

        def y_index(t):
            local = nbr_ref[b, t] - me * count + RIM
            local = jnp.where(local < 0, local + blocks, local)
            local = jnp.where(local >= blocks, local - blocks, local)
            local = jnp.clip(local - first, 0, side - 1) + (0 if i < RIM else side)
            return code_ref[b, t] * (2 * side) + local

        own = x_ref[RIM + i if i < RIM else side + EDGE - 2 * RIM + i]
        done_ref[i] = mixed_skip(y_ref, y_index, taps, mix_wide, mix_ref, own)
    copies = [
        pltpu.make_async_copy(done_ref.at[pl.ds(0, RIM)], skip_ref.at[pl.ds(0, RIM)], sem.at[0]),
        pltpu.make_async_copy(done_ref.at[pl.ds(RIM, RIM)], skip_ref.at[pl.ds(count - RIM, RIM)], sem.at[1]),
    ]
    for copy in copies:
        copy.start()
    products = dot(done_ref[...].reshape(2 * RIM * channels, cells), stacked)
    for d in range(tiles):
        counts_ref[d] = 0
    for b in range(count):
        dest = lax.div(route_ref[0, me * count + b], count)
        rank = next_rank(counts_ref, dest)
        if b in outer:
            i = outer.index(b)
            hop = lax.rem(dest - me + tiles, tiles)
            place(
                acc_ref, hop * halves, products[i * channels:(i + 1) * channels],
                rcode_ref[0, b], rank, cq,
            )
    lane = lax.broadcasted_iota(jnp.int32, (channels // 2, LANES), 1)
    half = LANES // 2
    for hop in range(tiles):
        out = out_refs[hop]
        row = 0
        for h in range(halves):
            value = acc_ref[hop * halves + h]
            if out.shape[0] - row >= channels:
                out[row:row + channels] = value.astype(BF16)
                row += channels
            else:
                low = pltpu.roll(value[channels // 2:], half, axis=1)
                out[row:] = jnp.where(lane < half, value[:channels // 2], low).astype(BF16)
    for copy in copies:
        copy.wait()


def route_slots(route_ref, slots_ref, count):
    tiles = route_ref.shape[1] // count
    per = count // tiles
    me = lax.axis_index("tile")
    for hop in range(tiles):
        source = lax.rem(me - hop + tiles, tiles)
        at = hop * per
        for b in range(count):
            slot = route_ref[0, source * count + b] - me * count
            slots_ref[at] = slot
            at = at + jnp.where((slot >= 0) & (slot < count), 1, 0)


def prepare_kernel(count, route_ref, late_ref, slots_ref):
    del late_ref
    route_slots(route_ref, slots_ref, count)


def merge_kernel(cq, slots_ref, *refs):
    sent_refs, (coarse_ref, first_ref, last_ref, acc_ref) = refs[:-4], refs[-4:]
    tiles = len(sent_refs)
    blocks, channels, cells = coarse_ref.shape
    per_block = cells // cq
    per = blocks * per_block // tiles
    lanes = LANES // cq
    half = LANES // 2
    lane = lax.broadcasted_iota(jnp.int32, (channels, LANES), 1)
    group = lax.div(lane, cq)
    for hop, sent in enumerate(sent_refs):
        for rank in range(per):
            row = rank // lanes * channels
            if sent.shape[0] - row >= channels:
                piece = sent[row:row + channels].astype(F32)
            else:
                packed = sent[row:].astype(F32)
                piece = jnp.concatenate([packed, pltpu.roll(packed, half, axis=1)], axis=0)
            slot = slots_ref[hop * per + rank]
            target = lax.rem(slot, lanes)
            amount = lax.rem((target - rank % lanes) * cq + LANES, LANES)
            at = lax.div(slot, lanes)
            acc_ref[at] = jnp.where(group == target, pltpu.roll(piece, amount, axis=1), acc_ref[at])
    parts = cells // LANES
    for c in range(blocks):
        value = jnp.concatenate([acc_ref[c * parts + h] for h in range(parts)], axis=1).astype(BF16)
        coarse_ref[c] = value
        if c == 0:
            first_ref[...] = value
        if c == blocks - 1:
            last_ref[...] = value


def coarse_kernel(code_ref, coarse_ref, left_ref, right_ref, seam_ref, spatial_ref, mix_ref, out_ref):
    blocks = coarse_ref.shape[0]
    mix_wide = joined_mix(mix_ref, mix_ref.shape[0])
    for c in range(blocks):
        own = coarse_ref[c]
        beside = [
            left_ref[...] if c == 0 else coarse_ref[c - 1],
            right_ref[...] if c == blocks - 1 else coarse_ref[c + 1],
            seam_ref[c],
        ]
        edges = [dot(rows, spatial_ref[code_ref[c, e]]).astype(BF16) for e, rows in enumerate(beside)]
        total = dot(mix_wide, jnp.concatenate([own] + edges, axis=0))
        out_ref[c] = (own.astype(F32) + silu(total)).astype(BF16)


def params(**more):
    return pltpu.CompilerParams(vmem_limit_bytes=VMEM_BYTES, **more)


def per_device(
    fine, conv_spatial, conv_mix, neighbours, fine_codes, restrict, restrict_codes, route,
    coarse_spatial, coarse_mix, coarse_codes,
):
    x = fine[0, 0]
    count, channels, cells = x.shape
    rotations = conv_spatial.shape[0]
    cq = restrict.shape[2]
    tiles = route.shape[1] // count
    per = count // tiles
    halves = -(-per * cq // LANES)
    left_over = per * cq % LANES
    sent_rows = per * cq // LANES * channels
    if left_over:
        sent_rows += channels // 2 if left_over <= LANES // 2 else channels
    blocks = count * cq // cells
    nbr, codes = neighbours[0], fine_codes[0]

    before = shifted(x[count - RIM:], "tile", 1)
    after = shifted(x[:RIM], "tile", -1)
    skip, acc = pl.pallas_call(
        inner_kernel,
        out_shape=(
            jax.ShapeDtypeStruct(x.shape, BF16),
            jax.ShapeDtypeStruct((tiles * halves, channels, LANES), F32),
        ),
        in_specs=[SMEM()] * 4 + [VMEM()] * 4,
        out_specs=(VMEM(), VMEM()),
        scratch_shapes=[
            pltpu.VMEM((rotations * count, channels, cells), BF16),
            pltpu.SMEM((tiles,), jnp.int32),
        ],
        compiler_params=params(),
        cost_estimate=pl.CostEstimate(flops=4 * 10**9, bytes_accessed=4 * 10**6, transcendentals=10**6),
        name="inner",
    )(nbr, codes, restrict_codes, route, x, conv_spatial, conv_mix, restrict)

    side = EDGE + RIM
    whole = pl.BlockSpec((RIM, channels, cells), lambda i: (0, 0, 0))

    def full(a):
        return pl.BlockSpec(a.shape, lambda i: (0,) * a.ndim)

    sent_shape = jax.ShapeDtypeStruct((sent_rows, LANES), BF16)
    skip, *sent = pl.pallas_call(
        rim_kernel,
        grid=(1,),
        out_shape=(jax.ShapeDtypeStruct(x.shape, BF16),) + (sent_shape,) * tiles,
        in_specs=[SMEM()] * 4
        + [
            whole,
            pl.BlockSpec((EDGE, channels, cells), lambda i: (0, 0, 0)),
            pl.BlockSpec((EDGE, channels, cells), lambda i: (count // EDGE - 1, 0, 0)),
            whole,
            full(conv_spatial),
            full(conv_mix),
            full(restrict),
            full(acc),
            ANY(),
        ],
        out_specs=(ANY(),) + (pl.BlockSpec((sent_rows, LANES), lambda i: (0, 0)),) * tiles,
        scratch_shapes=[
            pltpu.VMEM(acc.shape, F32),
            pltpu.VMEM((2 * side, channels, cells), BF16),
            pltpu.VMEM((rotations * 2 * side, channels, cells), BF16),
            pltpu.VMEM((2 * RIM, channels, cells), BF16),
            pltpu.SMEM((tiles,), jnp.int32),
            pltpu.SemaphoreType.DMA((2,)),
        ],
        input_output_aliases={12: 0},
        compiler_params=params(),
        name="rim",
    )(nbr, codes, restrict_codes, route, before, x, x, after, conv_spatial, conv_mix, restrict, acc, skip)

    slots = pl.pallas_call(
        functools.partial(prepare_kernel, count),
        out_shape=jax.ShapeDtypeStruct((count + 1,), jnp.int32),
        in_specs=[SMEM(), ANY()],
        out_specs=SMEM(),
        name="slots",
    )(route, sent[0])
    arrived = [sent[0]] + [shifted(sent[hop], "tile", hop) for hop in range(1, tiles)]

    block_shape = jax.ShapeDtypeStruct((channels, cells), BF16)
    coarse, first, last = pl.pallas_call(
        functools.partial(merge_kernel, cq),
        out_shape=(jax.ShapeDtypeStruct((blocks, channels, cells), BF16), block_shape, block_shape),
        in_specs=[SMEM()] + [VMEM()] * tiles,
        out_specs=(VMEM(), VMEM(), VMEM()),
        scratch_shapes=[pltpu.VMEM((blocks * cells // LANES, channels, LANES), F32)],
        compiler_params=params(),
        name="merge",
    )(slots, *arrived)

    left = shifted(last, "tile", 1)
    right = shifted(first, "tile", -1)
    seam = shifted(coarse, "sect", 1)
    coarse_out = pl.pallas_call(
        coarse_kernel,
        out_shape=jax.ShapeDtypeStruct(coarse.shape, BF16),
        in_specs=[SMEM()] + [VMEM()] * 6,
        out_specs=VMEM(),
        compiler_params=params(),
        name="coarse",
    )(coarse_codes[0], coarse, left, right, seam, coarse_spatial, coarse_mix)
    return (skip[None, None], coarse_out[None, None])


def solution(mesh):
    data = P(("groups", "chan"), "sect", "tile", None, None)
    placed = (
        data,
        P(),
        P(),
        P("sect", "tile", None),
        P("sect", "tile", None),
        P(),
        P("sect", "tile"),
        P("sect", None),
        P(),
        P(),
        P("sect", "tile", None),
    )
    return jax.shard_map(
        per_device, mesh=mesh, in_specs=placed, out_specs=(data, data), check_vma=False
    )
```

```python
import functools

import jax
import jax.numpy as jnp
from jax import lax
from jax.experimental import pallas as pl
from jax.experimental.pallas import tpu as pltpu
from jax.sharding import PartitionSpec as P

LANES = 128
RIM = 2
CHUNK = 8
VMEM_MIB = 40

SMEM = functools.partial(pl.BlockSpec, memory_space=pltpu.SMEM)
VMEM = functools.partial(pl.BlockSpec, memory_space=pltpu.VMEM)
ANY = functools.partial(pl.BlockSpec, memory_space=pl.ANY)
F32 = jnp.float32
BF16 = jnp.bfloat16


def dot(a, b):
    return jnp.dot(a, b, preferred_element_type=F32)


def silu(v):
    return v * (0.5 + 0.5 * jnp.tanh(0.5 * v))


def shifted(value, axis, steps):
    count = lax.axis_size(axis)
    return lax.ppermute(value, axis, [(i, (i + steps) % count) for i in range(count)])


def joined_mix(mix_ref, terms):
    return jnp.concatenate([mix_ref[t] for t in range(terms)], axis=1)


def dot_t(a, b):
    return lax.dot_general(a, b, (((1,), (1,)), ((), ())), preferred_element_type=F32)


def swapped(even, value, axis):
    count = lax.axis_size(axis)
    first = 0 if even else 1
    pairs = []
    for i in range(first, count + first, 2):
        here, there = i % count, (i + 1) % count
        pairs += [(here, there), (there, here)]
    return lax.ppermute(value, axis, pairs)


def faces_right():
    return lax.rem(lax.axis_index("tile"), 2) == 0


def mixed_skip(y_ref, y_index, taps, mix_wide, mix_ref, own):
    terms = [y_ref[y_index(t)] for t in range(taps)]
    wide = mix_wide.shape[1] // mix_ref.shape[1]
    mixed = dot(mix_wide, jnp.concatenate(terms[:wide], axis=0))
    for t in range(wide, taps):
        mixed = mixed + dot(mix_ref[t], terms[t])
    return (own.astype(F32) + silu(mixed)).astype(BF16)


def place(acc_ref, at, product, code, rank, cq):
    per = LANES // cq
    slot = lax.rem(rank, per)
    amount = lax.rem((slot - code) * cq + LANES, LANES)
    turned = pltpu.roll(product, amount, axis=1)
    lane = lax.broadcasted_iota(jnp.int32, turned.shape, 1)
    at = at + lax.div(rank, per)
    acc_ref[at] = jnp.where(lax.div(lane, cq) == slot, turned, acc_ref[at])


class Packing:
    def __init__(self, per, cq, channels):
        self.cq, self.channels = cq, channels
        self.lanes = LANES // cq
        self.full, left = divmod(per, self.lanes)
        self.half = 0 < left * 2 <= self.lanes
        if left and not self.half:
            self.full += 1
        self.parts = self.full + self.half
        self.rows = self.full * channels + (channels // 2 if self.half else 0)

    def width(self, tiles):
        return (tiles * self.full + (-(-tiles // 2) if self.half else 0)) * LANES

    def column(self, tiles, hop, rank):
        whole = (hop * self.full * self.lanes + rank) * self.cq
        if not self.half:
            return whole
        split = (
            (tiles * self.full + hop // 2) * LANES
            + hop % 2 * (LANES // 2)
            + (rank - self.full * self.lanes) * self.cq
        )
        return jnp.where(rank < self.full * self.lanes, whole, split)


def cut_kernel(x_ref, first_ref, second_ref, sems):
    count = x_ref.shape[0]
    right = faces_right()
    last = count - RIM
    copies = [
        pltpu.make_async_copy(x_ref.at[pl.ds(jnp.where(right, last, 0), RIM)], first_ref, sems.at[0]),
        pltpu.make_async_copy(x_ref.at[pl.ds(jnp.where(right, 0, last), RIM)], second_ref, sems.at[1]),
    ]
    for copy in copies:
        copy.start()
    for copy in copies:
        copy.wait()


def products_kernel(x_ref, spatial_ref, y_ref, rows_ref, table_ref, x_sems, table_sems):
    count, channels, cells = x_ref.shape
    rotations = spatial_ref.shape[0]
    extended = count + 2 * RIM
    steps = count // CHUNK
    tables = [
        pltpu.make_async_copy(spatial_ref.at[r], table_ref.at[r], table_sems.at[r]) for r in range(rotations)
    ]

    def fetch(step):
        part = pl.ds(step * CHUNK, CHUNK)
        return pltpu.make_async_copy(x_ref.at[part], rows_ref.at[part], x_sems.at[step])

    fetch(0).start()
    for table in tables:
        table.start()
    for step in range(1, steps):
        fetch(step).start()
    for table in tables:
        table.wait()

    @pl.loop(0, steps)
    def _(step):
        fetch(step).wait()
        rows = rows_ref[pl.ds(step * CHUNK, CHUNK)].reshape(CHUNK * channels, cells)
        for r in range(rotations):
            product = dot(rows, table_ref[r]).astype(BF16)
            y_ref[pl.ds(r * extended + RIM + step * CHUNK, CHUNK)] = product.reshape(CHUNK, channels, cells)


def fine_kernel(
    nbr_in, code_in, rcode_in, route_in, first_ref, second_ref, x_ref, spatial_ref, mix_ref, restrict_ref, y_in_ref,
    skip_ref, y_ref, *refs,
):
    sent_refs, refs = refs[:-14], refs[-14:]
    nbr_ref, code_ref, rcode_ref, route_ref, table_sems = refs[:5]
    acc_ref, x_own, table_ref, mix_own, restrict_own, done_ref, counts_ref, in_sems, out_sems = refs[5:]
    del y_in_ref
    count, channels, cells = x_ref.shape
    rotations, cq = restrict_ref.shape[:2]
    taps = mix_ref.shape[0]
    blocks = route_ref.shape[1]
    tiles = blocks // count
    extended = count + 2 * RIM
    parts = acc_ref.shape[0] // tiles
    packing = Packing(count // tiles, cq, channels)
    me = lax.axis_index("tile")
    fetches = [
        pltpu.make_async_copy(spatial_ref, table_ref, in_sems.at[0]),
        pltpu.make_async_copy(mix_ref, mix_own, in_sems.at[1]),
        pltpu.make_async_copy(restrict_ref, restrict_own, in_sems.at[2]),
        pltpu.make_async_copy(x_ref, x_own, in_sems.at[3]),
    ]
    tables = [
        pltpu.make_async_copy(source, target, table_sems.at[i])
        for i, (source, target) in enumerate(
            [(nbr_in, nbr_ref), (code_in, code_ref), (rcode_in, rcode_ref), (route_in, route_ref)]
        )
    ]
    for fetch in fetches + tables:
        fetch.start()
    acc_ref[...] = jnp.zeros(acc_ref.shape, F32)
    for d in range(tiles):
        counts_ref[d] = 0
    right = faces_right()
    received = [first_ref[...], second_ref[...]]
    before = jnp.where(right, received[1], received[0])
    after = jnp.where(right, received[0], received[1])
    halo = jnp.concatenate([before, after], axis=0).reshape(2 * RIM * channels, cells)
    fetches[0].wait()
    for r in range(rotations):
        product = dot(halo, table_ref[r]).astype(BF16).reshape(2 * RIM, channels, cells)
        y_ref[r * extended:r * extended + RIM] = product[:RIM]
        y_ref[r * extended + RIM + count:(r + 1) * extended] = product[RIM:]
    for fetch in fetches[1:] + tables:
        fetch.wait()
    mix_wide = joined_mix(mix_own, min(taps, cells // channels))
    restricts = restrict_own[...].reshape(rotations * cq, cells)
    stacked = jnp.concatenate([restricts] * (LANES // (rotations * cq)), axis=0)

    def put(step):
        part = pl.ds(step * CHUNK, CHUNK)
        return pltpu.make_async_copy(done_ref.at[part], skip_ref.at[part], out_sems.at[step])

    @pl.loop(0, count // CHUNK)
    def _(step):
        base = step * CHUNK
        for i in range(CHUNK):
            b = base + i

            def y_index(t):
                local = nbr_ref[t, 0, b] - me * count + RIM
                local = jnp.where(local < 0, local + blocks, local)
                local = jnp.where(local >= blocks, local - blocks, local)
                return code_ref[t, 0, b] * extended + local

            done_ref[b] = mixed_skip(y_ref, y_index, taps, mix_wide, mix_own, x_own[b])
        put(step).start()
        rows = done_ref[pl.ds(base, CHUNK)].reshape(CHUNK * channels, cells)
        products = dot_t(rows, stacked)
        for i in range(CHUNK):
            b = base + i
            dest = lax.div(route_ref[0, me * count + b], count)
            rank = counts_ref[dest]
            counts_ref[dest] = rank + 1
            hop = lax.rem(dest - me + tiles, tiles)
            place(
                acc_ref, hop * parts, products[i * channels:(i + 1) * channels],
                rcode_ref[0, b], rank, cq,
            )

    half = LANES // 2
    lane = lax.broadcasted_iota(jnp.int32, (channels // 2, LANES), 1)
    for hop in range(tiles):
        out = sent_refs[hop]
        for p in range(packing.full):
            out[p * channels:(p + 1) * channels] = acc_ref[hop * parts + p].astype(BF16)
        if packing.half:
            value = acc_ref[hop * parts + packing.full]
            lower = pltpu.roll(value[channels // 2:], half, axis=1)
            joined = jnp.where(lane < half, value[:channels // 2], lower)
            out[packing.full * channels:] = joined.astype(BF16)

    @pl.loop(0, count // CHUNK)
    def _(step):
        put(step).wait()


def order_kernel(count, cq, channels, route_ref, late_ref, order_ref):
    del late_ref
    blocks = route_ref.shape[1]
    tiles = blocks // count
    packing = Packing(count // tiles, cq, channels)
    me = lax.axis_index("tile")
    base = me * count
    route = route_ref[...]
    mine = jnp.where((route >= base) & (route < base + count), 1.0, 0.0)
    shape = (blocks, blocks)
    of, at = (lax.broadcasted_iota(jnp.int32, shape, d) for d in (0, 1))
    earlier = jnp.where((of < at) & (lax.div(of, count) == lax.div(at, count)), 1.0, 0.0)
    rank = dot(jnp.broadcast_to(mine, (8, blocks)).astype(BF16), earlier.astype(BF16))[:1].astype(jnp.int32)
    source = lax.div(lax.broadcasted_iota(jnp.int32, (1, blocks), 1), count)
    hop = lax.rem(me - source + tiles, tiles)
    column = packing.column(tiles, hop, rank).astype(F32)
    cells = count * cq
    cell = lax.broadcasted_iota(jnp.int32, (cells, blocks), 0)
    found = jnp.where(route == base + lax.div(cell, cq), column, 0.0)
    wanted = jnp.sum(found, axis=1, keepdims=True)
    wanted = wanted + lax.rem(lax.broadcasted_iota(jnp.int32, (cells, 1), 0), cq).astype(F32)
    across = jnp.transpose(jnp.broadcast_to(wanted, (cells, LANES)))[:1].astype(jnp.int32)
    step = LANES
    for row in range(0, order_ref.shape[0], step):
        index = row + lax.broadcasted_iota(jnp.int32, (step, cells), 0)
        order_ref[row:row + step] = jnp.where(index == across, 1.0, 0.0).astype(BF16)


def merge_kernel(per, cq, order_ref, *refs):
    arrived, (coarse_ref, first_ref, second_ref) = refs[:-3], refs[-3:]
    blocks, channels, cells = coarse_ref.shape
    tiles = len(arrived)
    packing = Packing(per, cq, channels)
    columns = [ref[p * channels:(p + 1) * channels] for ref in arrived for p in range(packing.full)]
    if packing.half:
        half = LANES // 2
        lane = lax.broadcasted_iota(jnp.int32, (channels // 2, LANES), 1)
        halves = [ref[packing.full * channels:].astype(F32) for ref in arrived]
        halves += [jnp.zeros_like(halves[0])] * (tiles % 2)
        for one, other in zip(halves[::2], halves[1::2]):
            upper = jnp.where(lane < half, one, pltpu.roll(other, half, axis=1))
            lower = jnp.where(lane < half, pltpu.roll(one, half, axis=1), other)
            columns.append(jnp.concatenate([upper, lower], axis=0).astype(BF16))
    joined = jnp.concatenate(columns, axis=1)
    values = [
        dot(joined, order_ref[:, c * cells:(c + 1) * cells]).astype(BF16) for c in range(blocks)
    ]
    for c in range(blocks):
        coarse_ref[c] = values[c]
    right = faces_right()
    first_ref[...] = jnp.where(right, values[-1], values[0])
    second_ref[...] = jnp.where(right, values[0], values[-1])


def coarse_kernel(code_ref, coarse_ref, first_ref, second_ref, seam_ref, spatial_ref, mix_ref, out_ref):
    blocks = coarse_ref.shape[0]
    right = faces_right()
    left_rows = jnp.where(right, second_ref[...], first_ref[...])
    right_rows = jnp.where(right, first_ref[...], second_ref[...])
    mix_wide = joined_mix(mix_ref, mix_ref.shape[0])
    for c in range(blocks):
        own = coarse_ref[c]
        beside = [
            left_rows if c == 0 else coarse_ref[c - 1],
            right_rows if c == blocks - 1 else coarse_ref[c + 1],
            seam_ref[c],
        ]
        edges = [dot(rows, spatial_ref[code_ref[c, 0, e]]).astype(BF16) for e, rows in enumerate(beside)]
        total = dot(mix_wide, jnp.concatenate([own] + edges, axis=0))
        out_ref[c] = (own.astype(F32) + silu(total)).astype(BF16)


def params(mib=VMEM_MIB):
    return pltpu.CompilerParams(vmem_limit_bytes=mib * 1024 * 1024)


def per_device(
    fine, conv_spatial, conv_mix, neighbours, fine_codes, restrict, restrict_codes, route,
    coarse_spatial, coarse_mix, coarse_codes,
):
    x = fine[0, 0]
    count, channels, cells = x.shape
    rotations = conv_spatial.shape[0]
    cq = restrict.shape[2]
    tiles = route.shape[1] // count
    per = count // tiles
    blocks = count * cq // cells
    packing = Packing(per, cq, channels)
    nbr, codes = neighbours.transpose(2, 0, 1), fine_codes.transpose(2, 0, 1)
    narrow = restrict.transpose(0, 2, 1)

    rim_shape = jax.ShapeDtypeStruct((RIM, channels, cells), BF16)
    first, second = pl.pallas_call(
        cut_kernel,
        out_shape=(rim_shape, rim_shape),
        in_specs=[ANY()],
        out_specs=(VMEM(), VMEM()),
        scratch_shapes=[pltpu.SemaphoreType.DMA((2,))],
        name="cut",
    )(x)
    first = swapped(True, first, "tile")
    second = swapped(False, second, "tile")

    y_shape = (rotations * (count + 2 * RIM), channels, cells)
    steps = count // CHUNK
    y = pl.pallas_call(
        products_kernel,
        out_shape=jax.ShapeDtypeStruct(y_shape, BF16),
        in_specs=[ANY(), ANY()],
        out_specs=VMEM(),
        scratch_shapes=[
            pltpu.VMEM(x.shape, BF16),
            pltpu.VMEM(conv_spatial.shape, BF16),
            pltpu.SemaphoreType.DMA((steps,)),
            pltpu.SemaphoreType.DMA((rotations,)),
        ],
        compiler_params=params(),
        cost_estimate=pl.CostEstimate(flops=4 * 10**9, bytes_accessed=4 * 10**6, transcendentals=10**6),
        name="products",
    )(x, conv_spatial)

    sent_shape = jax.ShapeDtypeStruct((packing.rows, LANES), BF16)
    skip, _, *sent = pl.pallas_call(
        fine_kernel,
        out_shape=(jax.ShapeDtypeStruct(x.shape, BF16), jax.ShapeDtypeStruct(y_shape, BF16)) + (sent_shape,) * tiles,
        in_specs=[ANY()] * 4 + [VMEM()] * 2 + [ANY()] * 4 + [VMEM()],
        out_specs=(ANY(), VMEM()) + (VMEM(),) * tiles,
        scratch_shapes=[pltpu.SMEM(a.shape, jnp.int32) for a in (nbr, codes, restrict_codes, route)]
        + [
            pltpu.SemaphoreType.DMA((4,)),
            pltpu.VMEM((tiles * packing.parts, channels, LANES), F32),
            pltpu.VMEM(x.shape, BF16),
            pltpu.VMEM(conv_spatial.shape, BF16),
            pltpu.VMEM(conv_mix.shape, BF16),
            pltpu.VMEM(narrow.shape, BF16),
            pltpu.VMEM(x.shape, BF16),
            pltpu.SMEM((tiles,), jnp.int32),
            pltpu.SemaphoreType.DMA((4,)),
            pltpu.SemaphoreType.DMA((steps,)),
        ],
        input_output_aliases={10: 1},
        compiler_params=params(),
        name="fine",
    )(nbr, codes, restrict_codes, route, first, second, x, conv_spatial, conv_mix, narrow, y)

    order = pl.pallas_call(
        functools.partial(order_kernel, count, cq, channels),
        out_shape=jax.ShapeDtypeStruct((packing.width(tiles), count * cq), BF16),
        in_specs=[VMEM(), VMEM()],
        out_specs=VMEM(),
        compiler_params=params(),
        name="order",
    )(route, sent[0])
    arrived = [sent[0]] + [shifted(sent[hop], "tile", hop) for hop in range(1, tiles)]

    block_shape = jax.ShapeDtypeStruct((channels, cells), BF16)
    coarse, first, second = pl.pallas_call(
        functools.partial(merge_kernel, per, cq),
        out_shape=(jax.ShapeDtypeStruct((blocks, channels, cells), BF16), block_shape, block_shape),
        in_specs=[VMEM()] * (1 + tiles),
        out_specs=(VMEM(), VMEM(), VMEM()),
        compiler_params=params(),
        name="merge",
    )(order, *arrived)

    first = swapped(True, first, "tile")
    second = swapped(False, second, "tile")
    seam = shifted(coarse, "sect", 1)
    coarse_out = pl.pallas_call(
        coarse_kernel,
        out_shape=jax.ShapeDtypeStruct(coarse.shape, BF16),
        in_specs=[SMEM()] + [VMEM()] * 6,
        out_specs=VMEM(),
        compiler_params=params(),
        name="coarse",
    )(coarse_codes.transpose(1, 0, 2), coarse, first, second, seam, coarse_spatial, coarse_mix)
    return (skip[None, None], coarse_out[None, None])


def solution(mesh):
    data = P(("groups", "chan"), "sect", "tile", None, None)
    placed = (
        data,
        P(),
        P(),
        P("sect", "tile", None),
        P("sect", "tile", None),
        P(),
        P("sect", "tile"),
        P("sect", None),
        P(),
        P(),
        P("sect", "tile", None),
    )
    return jax.shard_map(
        per_device, mesh=mesh, in_specs=placed, out_specs=(data, data), check_vma=False
    )
```

```python
import functools

import jax
import jax.numpy as jnp
from jax import lax
from jax.experimental import pallas as pl
from jax.experimental.pallas import tpu as pltpu
from jax.sharding import PartitionSpec as P

LANES = 128
RIM = 2
CHUNK = 8
EARLY = 3
VMEM_MIB = 40

SMEM = functools.partial(pl.BlockSpec, memory_space=pltpu.SMEM)
VMEM = functools.partial(pl.BlockSpec, memory_space=pltpu.VMEM)
ANY = functools.partial(pl.BlockSpec, memory_space=pl.ANY)
HBM = functools.partial(pl.BlockSpec, memory_space=pltpu.HBM)
F32 = jnp.float32
BF16 = jnp.bfloat16


def dot(a, b):
    return jnp.dot(a, b, preferred_element_type=F32)


def silu(v):
    return v * (0.5 + 0.5 * jnp.tanh(0.5 * v))


def shifted(value, axis, steps):
    count = lax.axis_size(axis)
    return lax.ppermute(value, axis, [(i, (i + steps) % count) for i in range(count)])


def joined_mix(mix_ref, terms):
    return jnp.concatenate([mix_ref[t] for t in range(terms)], axis=1)


def dot_t(a, b):
    return lax.dot_general(a, b, (((1,), (1,)), ((), ())), preferred_element_type=F32)


def swapped(even, value, axis):
    count = lax.axis_size(axis)
    first = 0 if even else 1
    pairs = []
    for i in range(first, count + first, 2):
        here, there = i % count, (i + 1) % count
        pairs += [(here, there), (there, here)]
    return lax.ppermute(value, axis, pairs)


def faces_right():
    return lax.rem(lax.axis_index("tile"), 2) == 0


def mixed_skip(y_ref, y_index, taps, mix_wide, mix_ref, own):
    terms = [y_ref[y_index(t)] for t in range(taps)]
    wide = mix_wide.shape[1] // mix_ref.shape[1]
    mixed = dot(mix_wide, jnp.concatenate(terms[:wide], axis=0))
    for t in range(wide, taps):
        mixed = mixed + dot(mix_ref[t], terms[t])
    return (own.astype(F32) + silu(mixed)).astype(BF16)


def place(acc_ref, at, product, code, rank, cq):
    per = LANES // cq
    slot = lax.rem(rank, per)
    amount = lax.rem((slot - code) * cq + LANES, LANES)
    turned = pltpu.roll(product, amount, axis=1)
    lane = lax.broadcasted_iota(jnp.int32, turned.shape, 1)
    at = at + lax.div(rank, per)
    acc_ref[at] = jnp.where(lax.div(lane, cq) == slot, turned, acc_ref[at])


class Packing:
    def __init__(self, per, cq, channels):
        self.cq, self.channels = cq, channels
        self.lanes = LANES // cq
        self.full, left = divmod(per, self.lanes)
        self.half = 0 < left * 2 <= self.lanes
        if left and not self.half:
            self.full += 1
        self.parts = self.full + self.half
        self.rows = self.full * channels + (channels // 2 if self.half else 0)

    def width(self, tiles):
        return (tiles * self.full + (-(-tiles // 2) if self.half else 0)) * LANES

    def column(self, tiles, hop, rank):
        whole = (hop * self.full * self.lanes + rank) * self.cq
        if not self.half:
            return whole
        split = (
            (tiles * self.full + hop // 2) * LANES
            + hop % 2 * (LANES // 2)
            + (rank - self.full * self.lanes) * self.cq
        )
        return jnp.where(rank < self.full * self.lanes, whole, split)


def cut_kernel(x_ref, first_ref, second_ref, sems):
    right = faces_right()
    last = x_ref.shape[0] - RIM
    copies = [
        pltpu.make_async_copy(x_ref.at[pl.ds(jnp.where(right, last, 0), RIM)], first_ref, sems.at[0]),
        pltpu.make_async_copy(x_ref.at[pl.ds(jnp.where(right, 0, last), RIM)], second_ref, sems.at[1]),
    ]
    for copy in copies:
        copy.start()
    for copy in copies:
        copy.wait()


class Level:
    def __init__(self, tables, y_ref, x_ref, mix_ref, restrict_ref, done_ref, acc_ref, counts_ref):
        self.nbr, self.code, self.rcode, self.route = tables
        self.y, self.x, self.mix, self.done, self.acc, self.counts = y_ref, x_ref, mix_ref, done_ref, acc_ref, counts_ref
        self.count, self.channels, self.cells = x_ref.shape
        self.rotations, self.cq = restrict_ref.shape[:2]
        self.taps = mix_ref.shape[0]
        self.blocks = self.route.shape[1]
        self.tiles = self.blocks // self.count
        self.extended = self.count + 2 * RIM
        self.me = lax.axis_index("tile")
        self.mix_wide = joined_mix(mix_ref, min(self.taps, self.cells // self.channels))
        restricts = restrict_ref[...].reshape(self.rotations * self.cq, self.cells)
        self.stacked = jnp.concatenate([restricts] * (LANES // (self.rotations * self.cq)), axis=0)
        for d in range(self.tiles):
            counts_ref[d] = 0

    def y_index(self, b, t):
        local = self.nbr[t, 0, b] - self.me * self.count + RIM
        local = jnp.where(local < 0, local + self.blocks, local)
        local = jnp.where(local >= self.blocks, local - self.blocks, local)
        return self.code[t, 0, b] * self.extended + local

    def pass_over(self, base, store=None):
        for i in range(CHUNK):
            b = base + i
            dest = lax.div(self.route[0, self.me * self.count + b], self.count)
            rank = self.counts[dest]
            self.counts[dest] = rank + 1
            if store is not None:
                store(i, b, dest, rank)

    def run(self, base):
        for i in range(CHUNK):
            b = base + i
            self.done[b] = mixed_skip(
                self.y, functools.partial(self.y_index, b), self.taps, self.mix_wide, self.mix, self.x[b]
            )

    def pack(self, base):
        rows = self.done[base:base + CHUNK].reshape(CHUNK * self.channels, self.cells)
        products = dot_t(rows, self.stacked)
        parts = self.acc.shape[0] // self.tiles

        def store(i, b, dest, rank):
            hop = lax.rem(dest - self.me + self.tiles, self.tiles)
            product = products[i * self.channels:(i + 1) * self.channels]
            place(self.acc, hop * parts, product, self.rcode[0, b], rank, self.cq)

        self.pass_over(base, store)


def fetched(sources, targets, sems):
    copies = [
        pltpu.make_async_copy(source, target, sems.at[i])
        for i, (source, target) in enumerate(zip(sources, targets))
    ]
    for copy in copies:
        copy.start()
    return copies


def chunks_of(count):
    return range(0, count, CHUNK)


def is_early(base, count):
    return CHUNK <= base < min((1 + EARLY) * CHUNK, count - CHUNK)


def put_of(done_ref, skip_ref, sems):
    def put(base):
        part = pl.ds(base, CHUNK)
        return pltpu.make_async_copy(done_ref.at[part], skip_ref.at[part], sems.at[base // CHUNK])

    return put


def early_kernel(
    x_ref, table_ref, nbr_ref, code_ref, rcode_ref, route_ref, mix_ref, restrict_ref,
    y_ref, skip_ref, acc_ref,
    nbr, code, rcode, route, mix, restrict, done_ref, counts_ref, in_sems, out_sems,
):
    count, channels, cells = x_ref.shape
    rotations = table_ref.shape[0]
    extended = count + 2 * RIM
    copies = fetched(
        (nbr_ref, code_ref, rcode_ref, route_ref, mix_ref, restrict_ref),
        (nbr, code, rcode, route, mix, restrict), in_sems,
    )
    acc_ref[...] = jnp.zeros(acc_ref.shape, F32)
    for base in chunks_of(count):
        rows = x_ref[base:base + CHUNK].reshape(CHUNK * channels, cells)
        for r in range(rotations):
            product = dot(rows, table_ref[r]).astype(BF16)
            y_ref[pl.ds(r * extended + RIM + base, CHUNK)] = product.reshape(CHUNK, channels, cells)
    for copy in copies:
        copy.wait()
    level = Level((nbr, code, rcode, route), y_ref, x_ref, mix, restrict, done_ref, acc_ref, counts_ref)
    put = put_of(done_ref, skip_ref, out_sems)
    for base in chunks_of(count):
        if is_early(base, count):
            level.run(base)
            put(base).start()
            level.pack(base)
        else:
            level.pass_over(base)
    for base in chunks_of(count):
        if is_early(base, count):
            put(base).wait()


def late_kernel(
    x_ref, table_ref, nbr_ref, code_ref, rcode_ref, route_ref, mix_ref, restrict_ref,
    first_ref, second_ref, y_in_ref, skip_in_ref, acc_in_ref, y_ref, skip_ref, acc_ref, *refs,
):
    sent_refs, refs = refs[:-10], refs[-10:]
    nbr, code, rcode, route, mix, restrict, done_ref, counts_ref, in_sems, out_sems = refs
    del y_in_ref, skip_in_ref, acc_in_ref
    count, channels, cells = x_ref.shape
    rotations = table_ref.shape[0]
    extended = count + 2 * RIM
    copies = fetched(
        (nbr_ref, code_ref, rcode_ref, route_ref, mix_ref, restrict_ref),
        (nbr, code, rcode, route, mix, restrict), in_sems,
    )
    right = faces_right()
    received = [first_ref[...], second_ref[...]]
    before = jnp.where(right, received[1], received[0])
    after = jnp.where(right, received[0], received[1])
    halo = jnp.concatenate([before, after], axis=0).reshape(2 * RIM * channels, cells)
    for r in range(rotations):
        product = dot(halo, table_ref[r]).astype(BF16).reshape(2 * RIM, channels, cells)
        y_ref[r * extended:r * extended + RIM] = product[:RIM]
        y_ref[r * extended + RIM + count:(r + 1) * extended] = product[RIM:]
    for copy in copies:
        copy.wait()
    level = Level((nbr, code, rcode, route), y_ref, x_ref, mix, restrict, done_ref, acc_ref, counts_ref)
    put = put_of(done_ref, skip_ref, out_sems)
    for base in chunks_of(count):
        if is_early(base, count):
            level.pass_over(base)
        else:
            level.run(base)
            put(base).start()
            level.pack(base)
    packing = Packing(count // level.tiles, level.cq, channels)
    half = LANES // 2
    lane = lax.broadcasted_iota(jnp.int32, (channels // 2, LANES), 1)
    for hop in range(level.tiles):
        out = sent_refs[hop]
        at = hop * packing.parts
        for p in range(packing.full):
            out[p * channels:(p + 1) * channels] = acc_ref[at + p].astype(BF16)
        if packing.half:
            value = acc_ref[at + packing.full]
            lower = pltpu.roll(value[channels // 2:], half, axis=1)
            joined = jnp.where(lane < half, value[:channels // 2], lower)
            out[packing.full * channels:] = joined.astype(BF16)
    for base in chunks_of(count):
        if not is_early(base, count):
            put(base).wait()


def order_kernel(count, cq, channels, route_ref, late_ref, order_ref):
    del late_ref
    blocks = route_ref.shape[1]
    tiles = blocks // count
    packing = Packing(count // tiles, cq, channels)
    me = lax.axis_index("tile")
    base = me * count
    route = route_ref[...]
    mine = jnp.where((route >= base) & (route < base + count), 1.0, 0.0)
    shape = (blocks, blocks)
    of, at = (lax.broadcasted_iota(jnp.int32, shape, d) for d in (0, 1))
    earlier = jnp.where((of < at) & (lax.div(of, count) == lax.div(at, count)), 1.0, 0.0)
    rank = dot(jnp.broadcast_to(mine, (8, blocks)).astype(BF16), earlier.astype(BF16))[:1].astype(jnp.int32)
    source = lax.div(lax.broadcasted_iota(jnp.int32, (1, blocks), 1), count)
    hop = lax.rem(me - source + tiles, tiles)
    column = packing.column(tiles, hop, rank).astype(F32)
    cells = count * cq
    cell = lax.broadcasted_iota(jnp.int32, (cells, blocks), 0)
    found = jnp.where(route == base + lax.div(cell, cq), column, 0.0)
    wanted = jnp.sum(found, axis=1, keepdims=True)
    wanted = wanted + lax.rem(lax.broadcasted_iota(jnp.int32, (cells, 1), 0), cq).astype(F32)
    across = jnp.transpose(jnp.broadcast_to(wanted, (cells, LANES)))[:1].astype(jnp.int32)
    step = LANES
    for row in range(0, order_ref.shape[0], step):
        index = row + lax.broadcasted_iota(jnp.int32, (step, cells), 0)
        order_ref[row:row + step] = jnp.where(index == across, 1.0, 0.0).astype(BF16)


def merge_kernel(per, cq, order_ref, *refs):
    arrived, (coarse_ref, first_ref, second_ref) = refs[:-3], refs[-3:]
    arrived = arrived[:1] + arrived[:0:-1]
    blocks, channels, cells = coarse_ref.shape
    tiles = len(arrived)
    packing = Packing(per, cq, channels)
    columns = [ref[p * channels:(p + 1) * channels] for ref in arrived for p in range(packing.full)]
    if packing.half:
        half = LANES // 2
        lane = lax.broadcasted_iota(jnp.int32, (channels // 2, LANES), 1)
        halves = [ref[packing.full * channels:].astype(F32) for ref in arrived]
        halves += [jnp.zeros_like(halves[0])] * (tiles % 2)
        for one, other in zip(halves[::2], halves[1::2]):
            upper = jnp.where(lane < half, one, pltpu.roll(other, half, axis=1))
            lower = jnp.where(lane < half, pltpu.roll(one, half, axis=1), other)
            columns.append(jnp.concatenate([upper, lower], axis=0).astype(BF16))
    joined = jnp.concatenate(columns, axis=1)
    values = [
        dot(joined, order_ref[:, c * cells:(c + 1) * cells]).astype(BF16) for c in range(blocks)
    ]
    for c in range(blocks):
        coarse_ref[c] = values[c]
    right = faces_right()
    first_ref[...] = jnp.where(right, values[-1], values[0])
    second_ref[...] = jnp.where(right, values[0], values[-1])


def inside_kernel(code_ref, coarse_ref, spatial_ref, mix_ref, total_ref, table_ref):
    blocks = coarse_ref.shape[0]
    values = [coarse_ref[c] for c in range(blocks)]
    for c in range(blocks):
        total = dot(mix_ref[0], values[c])
        for e, other in enumerate((c - 1, c + 1)):
            if 0 <= other < blocks:
                edge = dot(values[other], spatial_ref[code_ref[c, 0, e]]).astype(BF16)
                total = total + dot(mix_ref[e + 1], edge)
        total_ref[c] = total
        table_ref[2 + c] = spatial_ref[code_ref[c, 0, 2]]
    table_ref[0] = spatial_ref[code_ref[0, 0, 0]]
    table_ref[1] = spatial_ref[code_ref[blocks - 1, 0, 1]]


def coarse_kernel(seam_ref, first_ref, second_ref, coarse_ref, total_ref, table_ref, mix_ref, out_ref):
    blocks = coarse_ref.shape[0]
    right = faces_right()
    left_rows = jnp.where(right, second_ref[...], first_ref[...])
    right_rows = jnp.where(right, first_ref[...], second_ref[...])
    left_edge = dot(left_rows, table_ref[0]).astype(BF16)
    right_edge = dot(right_rows, table_ref[1]).astype(BF16)
    for c in range(blocks):
        total = total_ref[c] + dot(mix_ref[3], dot(seam_ref[c], table_ref[2 + c]).astype(BF16))
        if c == 0:
            total = total + dot(mix_ref[1], left_edge)
        if c == blocks - 1:
            total = total + dot(mix_ref[2], right_edge)
        out_ref[c] = (coarse_ref[c].astype(F32) + silu(total)).astype(BF16)


def params(mib=VMEM_MIB):
    return pltpu.CompilerParams(vmem_limit_bytes=mib * 1024 * 1024)


def per_device(
    fine, conv_spatial, conv_mix, neighbours, fine_codes, restrict, restrict_codes, route,
    coarse_spatial, coarse_mix, coarse_codes,
):
    x = fine[0, 0]
    count, channels, cells = x.shape
    rotations = conv_spatial.shape[0]
    cq = restrict.shape[2]
    tiles = route.shape[1] // count
    per = count // tiles
    blocks = count * cq // cells
    packing = Packing(per, cq, channels)
    nbr, codes = neighbours.transpose(2, 0, 1), fine_codes.transpose(2, 0, 1)
    narrow = restrict.transpose(0, 2, 1)

    rim_shape = jax.ShapeDtypeStruct((RIM, channels, cells), BF16)
    first, second = pl.pallas_call(
        cut_kernel,
        out_shape=(rim_shape, rim_shape),
        in_specs=[HBM()],
        out_specs=(VMEM(),) * 2,
        scratch_shapes=[pltpu.SemaphoreType.DMA((2,))],
        compiler_params=params(),
        cost_estimate=pl.CostEstimate(flops=4 * 10**9, bytes_accessed=10**6, transcendentals=0),
        name="cut",
    )(x)
    second = swapped(False, second, "tile")
    first = swapped(True, first, "tile")

    y_shape = (rotations * (count + 2 * RIM), channels, cells)
    steps = count // CHUNK
    tables = (nbr, codes, restrict_codes, route)
    shared = [pltpu.SMEM(a.shape, jnp.int32) for a in tables] + [
        pltpu.VMEM(conv_mix.shape, BF16),
        pltpu.VMEM(narrow.shape, BF16),
        pltpu.VMEM(x.shape, BF16),
        pltpu.SMEM((tiles,), jnp.int32),
        pltpu.SemaphoreType.DMA((6,)),
        pltpu.SemaphoreType.DMA((steps,)),
    ]
    made = (
        jax.ShapeDtypeStruct(y_shape, BF16),
        jax.ShapeDtypeStruct(x.shape, BF16),
        jax.ShapeDtypeStruct((tiles * packing.parts, channels, LANES), F32),
    )
    given = (x, conv_spatial) + tables + (conv_mix, narrow)
    given_specs = [VMEM()] * 2 + [ANY()] * 6
    y, skip, acc = pl.pallas_call(
        early_kernel,
        out_shape=made,
        in_specs=given_specs,
        out_specs=(VMEM(), ANY(), VMEM()),
        scratch_shapes=shared,
        compiler_params=params(),
        cost_estimate=pl.CostEstimate(flops=4 * 10**9, bytes_accessed=4 * 10**6, transcendentals=10**6),
        name="early",
    )(*given)

    sent_shape = jax.ShapeDtypeStruct((packing.rows, LANES), BF16)
    _, skip, _, *sent = pl.pallas_call(
        late_kernel,
        out_shape=made + (sent_shape,) * tiles,
        in_specs=given_specs + [VMEM()] * 3 + [ANY(), VMEM()],
        out_specs=(VMEM(), ANY(), VMEM()) + (VMEM(),) * tiles,
        scratch_shapes=shared,
        input_output_aliases={10: 0, 11: 1, 12: 2},
        compiler_params=params(),
        name="late",
    )(*given, first, second, y, skip, acc)

    order = pl.pallas_call(
        functools.partial(order_kernel, count, cq, channels),
        out_shape=jax.ShapeDtypeStruct((packing.width(tiles), count * cq), BF16),
        in_specs=[VMEM(), VMEM()],
        out_specs=VMEM(),
        compiler_params=params(),
        name="order",
    )(route, sent[0])
    arrived = [sent[0]] + [shifted(sent[hop], "tile", hop) for hop in range(1, tiles)]

    block_shape = jax.ShapeDtypeStruct((channels, cells), BF16)
    coarse, first, second = pl.pallas_call(
        functools.partial(merge_kernel, per, cq),
        out_shape=(jax.ShapeDtypeStruct((blocks, channels, cells), BF16), block_shape, block_shape),
        in_specs=[VMEM()] * (1 + tiles),
        out_specs=(VMEM(), VMEM(), VMEM()),
        compiler_params=params(),
        name="merge",
    )(order, arrived[0], *arrived[:0:-1])

    second = swapped(False, second, "tile")
    first = swapped(True, first, "tile")
    seam = shifted(coarse, "sect", 1)
    total, tables = pl.pallas_call(
        inside_kernel,
        out_shape=(
            jax.ShapeDtypeStruct(coarse.shape, F32),
            jax.ShapeDtypeStruct((2 + blocks,) + coarse_spatial.shape[1:], BF16),
        ),
        in_specs=[SMEM()] + [VMEM()] * 3,
        out_specs=(VMEM(), VMEM()),
        compiler_params=params(),
        name="inside",
    )(coarse_codes.transpose(1, 0, 2), coarse, coarse_spatial, coarse_mix)
    coarse_out = pl.pallas_call(
        coarse_kernel,
        out_shape=jax.ShapeDtypeStruct(coarse.shape, BF16),
        in_specs=[VMEM()] * 7,
        out_specs=VMEM(),
        compiler_params=params(),
        name="coarse",
    )(seam, first, second, coarse, total, tables, coarse_mix)
    return (skip[None, None], coarse_out[None, None])


def solution(mesh):
    data = P(("groups", "chan"), "sect", "tile", None, None)
    placed = (
        data,
        P(),
        P(),
        P("sect", "tile", None),
        P("sect", "tile", None),
        P(),
        P("sect", "tile"),
        P("sect", None),
        P(),
        P(),
        P("sect", "tile", None),
    )
    return jax.shard_map(
        per_device, mesh=mesh, in_specs=placed, out_specs=(data, data), check_vma=False
    )
```

```python
import functools

import jax
import jax.numpy as jnp
from jax import lax
from jax.experimental import pallas as pl
from jax.experimental.pallas import tpu as pltpu
from jax.sharding import PartitionSpec as P

LANES = 128
RIM = 2
CHUNK = 8
EARLY = 3
VMEM_MIB = 40

SMEM = functools.partial(pl.BlockSpec, memory_space=pltpu.SMEM)
VMEM = functools.partial(pl.BlockSpec, memory_space=pltpu.VMEM)
ANY = functools.partial(pl.BlockSpec, memory_space=pl.ANY)
HBM = functools.partial(pl.BlockSpec, memory_space=pltpu.HBM)
F32 = jnp.float32
BF16 = jnp.bfloat16


def dot(a, b):
    return jnp.dot(a, b, preferred_element_type=F32)


def silu(v):
    return v * (0.5 + 0.5 * jnp.tanh(0.5 * v))


def shifted(value, axis, steps):
    count = lax.axis_size(axis)
    return lax.ppermute(value, axis, [(i, (i + steps) % count) for i in range(count)])


def joined_mix(mix_ref, terms):
    return jnp.concatenate([mix_ref[t] for t in range(terms)], axis=1)


def dot_t(a, b):
    return lax.dot_general(a, b, (((1,), (1,)), ((), ())), preferred_element_type=F32)


def swapped(even, value, axis):
    count = lax.axis_size(axis)
    first = 0 if even else 1
    pairs = []
    for i in range(first, count + first, 2):
        here, there = i % count, (i + 1) % count
        pairs += [(here, there), (there, here)]
    return lax.ppermute(value, axis, pairs)


def paired(tiles):
    return tiles & (tiles - 1) == 0


def hop_between(dest, source, tiles):
    if paired(tiles):
        return lax.bitwise_xor(dest, source)
    return lax.rem(dest - source + tiles, tiles)


def exchanged(value, axis, hop):
    count = lax.axis_size(axis)
    pairs = [(i, i ^ hop if paired(count) else (i + hop) % count) for i in range(count)]
    return lax.ppermute(value, axis, pairs)


def hop_order(tiles):
    return list(range(tiles // 2, tiles)) + list(range(1, tiles // 2))


def faces_right():
    return lax.rem(lax.axis_index("tile"), 2) == 0


def mixed_skip(y_ref, y_index, taps, mix_wide, mix_ref, own):
    terms = [y_ref[y_index(t)] for t in range(taps)]
    wide = mix_wide.shape[1] // mix_ref.shape[1]
    mixed = dot(mix_wide, jnp.concatenate(terms[:wide], axis=0))
    for t in range(wide, taps):
        mixed = mixed + dot(mix_ref[t], terms[t])
    return (own.astype(F32) + silu(mixed)).astype(BF16)


def place(acc_ref, at, product, code, rank, cq):
    per = LANES // cq
    slot = lax.rem(rank, per)
    amount = lax.rem((slot - code) * cq + LANES, LANES)
    turned = pltpu.roll(product, amount, axis=1)
    lane = lax.broadcasted_iota(jnp.int32, turned.shape, 1)
    at = at + lax.div(rank, per)
    acc_ref[at] = jnp.where(lax.div(lane, cq) == slot, turned, acc_ref[at])


class Packing:
    def __init__(self, per, cq, channels):
        self.cq, self.channels = cq, channels
        self.lanes = LANES // cq
        self.full, left = divmod(per, self.lanes)
        self.half = 0 < left * 2 <= self.lanes
        if left and not self.half:
            self.full += 1
        self.parts = self.full + self.half
        self.rows = self.full * channels + (channels // 2 if self.half else 0)

    def width(self, tiles):
        return (tiles * self.full + (-(-tiles // 2) if self.half else 0)) * LANES

    def column(self, tiles, hop, rank):
        whole = (hop * self.full * self.lanes + rank) * self.cq
        if not self.half:
            return whole
        split = (
            (tiles * self.full + hop // 2) * LANES
            + hop % 2 * (LANES // 2)
            + (rank - self.full * self.lanes) * self.cq
        )
        return jnp.where(rank < self.full * self.lanes, whole, split)


def cut_kernel(x_ref, first_ref, second_ref, sems):
    right = faces_right()
    last = x_ref.shape[0] - RIM
    copies = [
        pltpu.make_async_copy(x_ref.at[pl.ds(jnp.where(right, last, 0), RIM)], first_ref, sems.at[0]),
        pltpu.make_async_copy(x_ref.at[pl.ds(jnp.where(right, 0, last), RIM)], second_ref, sems.at[1]),
    ]
    for copy in copies:
        copy.start()
    for copy in copies:
        copy.wait()


class Level:
    def __init__(self, tables, y_ref, x_ref, mix_ref, restrict_ref, done_ref, acc_ref, counts_ref):
        self.nbr, self.code, self.rcode, self.route = tables
        self.y, self.x, self.mix, self.done, self.acc, self.counts = y_ref, x_ref, mix_ref, done_ref, acc_ref, counts_ref
        self.count, self.channels, self.cells = x_ref.shape
        self.rotations, self.cq = restrict_ref.shape[:2]
        self.taps = mix_ref.shape[0]
        self.blocks = self.route.shape[1]
        self.tiles = self.blocks // self.count
        self.extended = self.count + 2 * RIM
        self.me = lax.axis_index("tile")
        self.mix_wide = joined_mix(mix_ref, min(self.taps, self.cells // self.channels))
        restricts = restrict_ref[...].reshape(self.rotations * self.cq, self.cells)
        self.stacked = jnp.concatenate([restricts] * (LANES // (self.rotations * self.cq)), axis=0)
        for d in range(self.tiles):
            counts_ref[d] = 0

    def y_index(self, b, t):
        local = self.nbr[t, 0, b] - self.me * self.count + RIM
        local = jnp.where(local < 0, local + self.blocks, local)
        local = jnp.where(local >= self.blocks, local - self.blocks, local)
        return self.code[t, 0, b] * self.extended + local

    def pass_over(self, base, store=None):
        for i in range(CHUNK):
            b = base + i
            dest = lax.div(self.route[0, self.me * self.count + b], self.count)
            rank = self.counts[dest]
            self.counts[dest] = rank + 1
            if store is not None:
                store(i, b, dest, rank)

    def run(self, base):
        for i in range(CHUNK):
            b = base + i
            self.done[b] = mixed_skip(
                self.y, functools.partial(self.y_index, b), self.taps, self.mix_wide, self.mix, self.x[b]
            )

    def pack(self, base):
        rows = self.done[base:base + CHUNK].reshape(CHUNK * self.channels, self.cells)
        products = dot_t(rows, self.stacked)
        parts = self.acc.shape[0] // self.tiles

        def store(i, b, dest, rank):
            hop = hop_between(dest, self.me, self.tiles)
            product = products[i * self.channels:(i + 1) * self.channels]
            place(self.acc, hop * parts, product, self.rcode[0, b], rank, self.cq)

        self.pass_over(base, store)


def fetched(sources, targets, sems):
    copies = [
        pltpu.make_async_copy(source, target, sems.at[i])
        for i, (source, target) in enumerate(zip(sources, targets))
    ]
    for copy in copies:
        copy.start()
    return copies


def chunks_of(count):
    return range(0, count, CHUNK)


def is_early(base, count):
    return CHUNK <= base < min((1 + EARLY) * CHUNK, count - CHUNK)


def put_of(done_ref, skip_ref, sems):
    def put(base):
        part = pl.ds(base, CHUNK)
        return pltpu.make_async_copy(done_ref.at[part], skip_ref.at[part], sems.at[base // CHUNK])

    return put


def early_kernel(
    x_ref, table_ref, nbr_ref, code_ref, rcode_ref, route_ref, mix_ref, restrict_ref,
    y_ref, skip_ref, acc_ref,
    nbr, code, rcode, route, mix, restrict, done_ref, counts_ref, in_sems, out_sems,
):
    count, channels, cells = x_ref.shape
    rotations = table_ref.shape[0]
    extended = count + 2 * RIM
    copies = fetched(
        (nbr_ref, code_ref, rcode_ref, route_ref, mix_ref, restrict_ref),
        (nbr, code, rcode, route, mix, restrict), in_sems,
    )
    acc_ref[...] = jnp.zeros(acc_ref.shape, F32)
    for base in chunks_of(count):
        rows = x_ref[base:base + CHUNK].reshape(CHUNK * channels, cells)
        for r in range(rotations):
            product = dot(rows, table_ref[r]).astype(BF16)
            y_ref[pl.ds(r * extended + RIM + base, CHUNK)] = product.reshape(CHUNK, channels, cells)
    for copy in copies:
        copy.wait()
    level = Level((nbr, code, rcode, route), y_ref, x_ref, mix, restrict, done_ref, acc_ref, counts_ref)
    put = put_of(done_ref, skip_ref, out_sems)
    for base in chunks_of(count):
        if is_early(base, count):
            level.run(base)
            put(base).start()
            level.pack(base)
        else:
            level.pass_over(base)
    for base in chunks_of(count):
        if is_early(base, count):
            put(base).wait()


def late_kernel(
    x_ref, table_ref, nbr_ref, code_ref, rcode_ref, route_ref, mix_ref, restrict_ref,
    first_ref, second_ref, y_in_ref, skip_in_ref, acc_in_ref, y_ref, skip_ref, acc_ref, *refs,
):
    sent_refs, refs = refs[:-10], refs[-10:]
    nbr, code, rcode, route, mix, restrict, done_ref, counts_ref, in_sems, out_sems = refs
    del y_in_ref, skip_in_ref, acc_in_ref
    count, channels, cells = x_ref.shape
    rotations = table_ref.shape[0]
    extended = count + 2 * RIM
    copies = fetched(
        (nbr_ref, code_ref, rcode_ref, route_ref, mix_ref, restrict_ref),
        (nbr, code, rcode, route, mix, restrict), in_sems,
    )
    right = faces_right()
    received = [first_ref[...], second_ref[...]]
    before = jnp.where(right, received[1], received[0])
    after = jnp.where(right, received[0], received[1])
    halo = jnp.concatenate([before, after], axis=0).reshape(2 * RIM * channels, cells)
    for r in range(rotations):
        product = dot(halo, table_ref[r]).astype(BF16).reshape(2 * RIM, channels, cells)
        y_ref[r * extended:r * extended + RIM] = product[:RIM]
        y_ref[r * extended + RIM + count:(r + 1) * extended] = product[RIM:]
    for copy in copies:
        copy.wait()
    level = Level((nbr, code, rcode, route), y_ref, x_ref, mix, restrict, done_ref, acc_ref, counts_ref)
    put = put_of(done_ref, skip_ref, out_sems)
    for base in chunks_of(count):
        if is_early(base, count):
            level.pass_over(base)
        else:
            level.run(base)
            put(base).start()
            level.pack(base)
    packing = Packing(count // level.tiles, level.cq, channels)
    half = LANES // 2
    lane = lax.broadcasted_iota(jnp.int32, (channels // 2, LANES), 1)
    for hop in range(level.tiles):
        out = sent_refs[hop]
        at = hop * packing.parts
        for p in range(packing.full):
            out[p * channels:(p + 1) * channels] = acc_ref[at + p].astype(BF16)
        if packing.half:
            value = acc_ref[at + packing.full]
            lower = pltpu.roll(value[channels // 2:], half, axis=1)
            joined = jnp.where(lane < half, value[:channels // 2], lower)
            out[packing.full * channels:] = joined.astype(BF16)
    for base in chunks_of(count):
        if not is_early(base, count):
            put(base).wait()


def order_kernel(count, cq, channels, route_ref, late_ref, order_ref):
    del late_ref
    blocks = route_ref.shape[1]
    tiles = blocks // count
    packing = Packing(count // tiles, cq, channels)
    me = lax.axis_index("tile")
    base = me * count
    route = route_ref[...]
    mine = jnp.where((route >= base) & (route < base + count), 1.0, 0.0)
    shape = (blocks, blocks)
    of, at = (lax.broadcasted_iota(jnp.int32, shape, d) for d in (0, 1))
    earlier = jnp.where((of < at) & (lax.div(of, count) == lax.div(at, count)), 1.0, 0.0)
    rank = dot(jnp.broadcast_to(mine, (8, blocks)).astype(BF16), earlier.astype(BF16))[:1].astype(jnp.int32)
    source = lax.div(lax.broadcasted_iota(jnp.int32, (1, blocks), 1), count)
    hop = hop_between(me, source, tiles)
    column = packing.column(tiles, hop, rank).astype(F32)
    cells = count * cq
    cell = lax.broadcasted_iota(jnp.int32, (cells, blocks), 0)
    found = jnp.where(route == base + lax.div(cell, cq), column, 0.0)
    wanted = jnp.sum(found, axis=1, keepdims=True)
    wanted = wanted + lax.rem(lax.broadcasted_iota(jnp.int32, (cells, 1), 0), cq).astype(F32)
    across = jnp.transpose(jnp.broadcast_to(wanted, (cells, LANES)))[:1].astype(jnp.int32)
    step = LANES
    for row in range(0, order_ref.shape[0], step):
        index = row + lax.broadcasted_iota(jnp.int32, (step, cells), 0)
        order_ref[row:row + step] = jnp.where(index == across, 1.0, 0.0).astype(BF16)


def merge_kernel(per, cq, order_ref, *refs):
    arrived, (coarse_ref, first_ref, second_ref) = refs[:-3], refs[-3:]
    order = hop_order(len(arrived))
    arrived = [arrived[0]] + [arrived[1 + order.index(hop)] for hop in range(1, len(arrived))]
    blocks, channels, cells = coarse_ref.shape
    tiles = len(arrived)
    packing = Packing(per, cq, channels)
    columns = [ref[p * channels:(p + 1) * channels] for ref in arrived for p in range(packing.full)]
    if packing.half:
        half = LANES // 2
        lane = lax.broadcasted_iota(jnp.int32, (channels // 2, LANES), 1)
        halves = [ref[packing.full * channels:].astype(F32) for ref in arrived]
        halves += [jnp.zeros_like(halves[0])] * (tiles % 2)
        for one, other in zip(halves[::2], halves[1::2]):
            upper = jnp.where(lane < half, one, pltpu.roll(other, half, axis=1))
            lower = jnp.where(lane < half, pltpu.roll(one, half, axis=1), other)
            columns.append(jnp.concatenate([upper, lower], axis=0).astype(BF16))
    joined = jnp.concatenate(columns, axis=1)
    values = [
        dot(joined, order_ref[:, c * cells:(c + 1) * cells]).astype(BF16) for c in range(blocks)
    ]
    for c in range(blocks):
        coarse_ref[c] = values[c]
    right = faces_right()
    first_ref[...] = jnp.where(right, values[-1], values[0])
    second_ref[...] = jnp.where(right, values[0], values[-1])


def inside_kernel(code_ref, coarse_ref, spatial_ref, mix_ref, total_ref, table_ref):
    blocks = coarse_ref.shape[0]
    values = [coarse_ref[c] for c in range(blocks)]
    for c in range(blocks):
        total = dot(mix_ref[0], values[c])
        for e, other in enumerate((c - 1, c + 1)):
            if 0 <= other < blocks:
                edge = dot(values[other], spatial_ref[code_ref[c, 0, e]]).astype(BF16)
                total = total + dot(mix_ref[e + 1], edge)
        total_ref[c] = total
        table_ref[2 + c] = spatial_ref[code_ref[c, 0, 2]]
    table_ref[0] = spatial_ref[code_ref[0, 0, 0]]
    table_ref[1] = spatial_ref[code_ref[blocks - 1, 0, 1]]


def coarse_kernel(seam_ref, first_ref, second_ref, coarse_ref, total_ref, table_ref, mix_ref, out_ref):
    blocks = coarse_ref.shape[0]
    right = faces_right()
    left_rows = jnp.where(right, second_ref[...], first_ref[...])
    right_rows = jnp.where(right, first_ref[...], second_ref[...])
    left_edge = dot(left_rows, table_ref[0]).astype(BF16)
    right_edge = dot(right_rows, table_ref[1]).astype(BF16)
    for c in range(blocks):
        total = total_ref[c] + dot(mix_ref[3], dot(seam_ref[c], table_ref[2 + c]).astype(BF16))
        if c == 0:
            total = total + dot(mix_ref[1], left_edge)
        if c == blocks - 1:
            total = total + dot(mix_ref[2], right_edge)
        out_ref[c] = (coarse_ref[c].astype(F32) + silu(total)).astype(BF16)


def params(mib=VMEM_MIB):
    return pltpu.CompilerParams(vmem_limit_bytes=mib * 1024 * 1024)


def per_device(
    fine, conv_spatial, conv_mix, neighbours, fine_codes, restrict, restrict_codes, route,
    coarse_spatial, coarse_mix, coarse_codes,
):
    x = fine[0, 0]
    count, channels, cells = x.shape
    rotations = conv_spatial.shape[0]
    cq = restrict.shape[2]
    tiles = route.shape[1] // count
    per = count // tiles
    blocks = count * cq // cells
    packing = Packing(per, cq, channels)
    nbr, codes = neighbours.transpose(2, 0, 1), fine_codes.transpose(2, 0, 1)
    narrow = restrict.transpose(0, 2, 1)

    rim_shape = jax.ShapeDtypeStruct((RIM, channels, cells), BF16)
    first, second = pl.pallas_call(
        cut_kernel,
        out_shape=(rim_shape, rim_shape),
        in_specs=[HBM()],
        out_specs=(VMEM(),) * 2,
        scratch_shapes=[pltpu.SemaphoreType.DMA((2,))],
        compiler_params=params(),
        cost_estimate=pl.CostEstimate(flops=4 * 10**9, bytes_accessed=10**6, transcendentals=0),
        name="cut",
    )(x)
    second = swapped(False, second, "tile")
    first = swapped(True, first, "tile")

    y_shape = (rotations * (count + 2 * RIM), channels, cells)
    steps = count // CHUNK
    tables = (nbr, codes, restrict_codes, route)
    shared = [pltpu.SMEM(a.shape, jnp.int32) for a in tables] + [
        pltpu.VMEM(conv_mix.shape, BF16),
        pltpu.VMEM(narrow.shape, BF16),
        pltpu.VMEM(x.shape, BF16),
        pltpu.SMEM((tiles,), jnp.int32),
        pltpu.SemaphoreType.DMA((6,)),
        pltpu.SemaphoreType.DMA((steps,)),
    ]
    made = (
        jax.ShapeDtypeStruct(y_shape, BF16),
        jax.ShapeDtypeStruct(x.shape, BF16),
        jax.ShapeDtypeStruct((tiles * packing.parts, channels, LANES), F32),
    )
    given = (x, conv_spatial) + tables + (conv_mix, narrow)
    given_specs = [VMEM()] * 2 + [ANY()] * 6
    y, skip, acc = pl.pallas_call(
        early_kernel,
        out_shape=made,
        in_specs=given_specs,
        out_specs=(VMEM(), ANY(), VMEM()),
        scratch_shapes=shared,
        compiler_params=params(),
        cost_estimate=pl.CostEstimate(flops=4 * 10**9, bytes_accessed=4 * 10**6, transcendentals=10**6),
        name="early",
    )(*given)

    sent_shape = jax.ShapeDtypeStruct((packing.rows, LANES), BF16)
    _, skip, _, *sent = pl.pallas_call(
        late_kernel,
        out_shape=made + (sent_shape,) * tiles,
        in_specs=given_specs + [VMEM()] * 3 + [ANY(), VMEM()],
        out_specs=(VMEM(), ANY(), VMEM()) + (VMEM(),) * tiles,
        scratch_shapes=shared,
        input_output_aliases={10: 0, 11: 1, 12: 2},
        compiler_params=params(),
        name="late",
    )(*given, first, second, y, skip, acc)

    order = pl.pallas_call(
        functools.partial(order_kernel, count, cq, channels),
        out_shape=jax.ShapeDtypeStruct((packing.width(tiles), count * cq), BF16),
        in_specs=[VMEM(), VMEM()],
        out_specs=VMEM(),
        compiler_params=params(),
        name="order",
    )(route, sent[0])
    arrived = [sent[0]] + [exchanged(sent[hop], "tile", hop) for hop in range(1, tiles)]

    block_shape = jax.ShapeDtypeStruct((channels, cells), BF16)
    coarse, first, second = pl.pallas_call(
        functools.partial(merge_kernel, per, cq),
        out_shape=(jax.ShapeDtypeStruct((blocks, channels, cells), BF16), block_shape, block_shape),
        in_specs=[VMEM()] * (1 + tiles),
        out_specs=(VMEM(), VMEM(), VMEM()),
        compiler_params=params(),
        name="merge",
    )(order, arrived[0], *[arrived[hop] for hop in hop_order(tiles)])

    second = swapped(False, second, "tile")
    first = swapped(True, first, "tile")
    seam = shifted(coarse, "sect", 1)
    total, tables = pl.pallas_call(
        inside_kernel,
        out_shape=(
            jax.ShapeDtypeStruct(coarse.shape, F32),
            jax.ShapeDtypeStruct((2 + blocks,) + coarse_spatial.shape[1:], BF16),
        ),
        in_specs=[SMEM()] + [VMEM()] * 3,
        out_specs=(VMEM(), VMEM()),
        compiler_params=params(),
        name="inside",
    )(coarse_codes.transpose(1, 0, 2), coarse, coarse_spatial, coarse_mix)
    coarse_out = pl.pallas_call(
        coarse_kernel,
        out_shape=jax.ShapeDtypeStruct(coarse.shape, BF16),
        in_specs=[VMEM()] * 7,
        out_specs=VMEM(),
        compiler_params=params(),
        name="coarse",
    )(seam, first, second, coarse, total, tables, coarse_mix)
    return (skip[None, None], coarse_out[None, None])


def solution(mesh):
    data = P(("groups", "chan"), "sect", "tile", None, None)
    placed = (
        data,
        P(),
        P(),
        P("sect", "tile", None),
        P("sect", "tile", None),
        P(),
        P("sect", "tile"),
        P("sect", None),
        P(),
        P(),
        P("sect", "tile", None),
    )
    return jax.shard_map(
        per_device, mesh=mesh, in_specs=placed, out_specs=(data, data), check_vma=False
    )
```

```python
import functools

import jax
import jax.numpy as jnp
from jax import lax
from jax.experimental import pallas as pl
from jax.experimental.pallas import tpu as pltpu
from jax.sharding import PartitionSpec as P

LANES = 128
RIM = 2
CHUNK = 8
EARLY = 4
VMEM_MIB = 40

SMEM = functools.partial(pl.BlockSpec, memory_space=pltpu.SMEM)
VMEM = functools.partial(pl.BlockSpec, memory_space=pltpu.VMEM)
ANY = functools.partial(pl.BlockSpec, memory_space=pl.ANY)
HBM = functools.partial(pl.BlockSpec, memory_space=pltpu.HBM)
F32 = jnp.float32
BF16 = jnp.bfloat16


def dot(a, b):
    return jnp.dot(a, b, preferred_element_type=F32)


def silu(v):
    return v * (0.5 + 0.5 * jnp.tanh(0.5 * v))


def shifted(value, axis, steps):
    count = lax.axis_size(axis)
    return lax.ppermute(value, axis, [(i, (i + steps) % count) for i in range(count)])


def joined_mix(mix_ref, terms):
    return jnp.concatenate([mix_ref[t] for t in range(terms)], axis=1)


def dot_t(a, b):
    return lax.dot_general(a, b, (((1,), (1,)), ((), ())), preferred_element_type=F32)


def swapped(even, value, axis):
    count = lax.axis_size(axis)
    first = 0 if even else 1
    pairs = []
    for i in range(first, count + first, 2):
        here, there = i % count, (i + 1) % count
        pairs += [(here, there), (there, here)]
    return lax.ppermute(value, axis, pairs)


def paired(tiles):
    return tiles & (tiles - 1) == 0


def hop_between(dest, source, tiles):
    if paired(tiles):
        return lax.bitwise_xor(dest, source)
    return lax.rem(dest - source + tiles, tiles)


def exchanged(value, axis, hop):
    count = lax.axis_size(axis)
    pairs = [(i, i ^ hop if paired(count) else (i + hop) % count) for i in range(count)]
    return lax.ppermute(value, axis, pairs)


def hop_order(tiles):
    return list(range(tiles // 2, tiles)) + list(range(1, tiles // 2))


def faces_right():
    return lax.rem(lax.axis_index("tile"), 2) == 0


def mixed_skip(y_ref, y_index, taps, mix_wide, mix_ref, own):
    terms = [y_ref[y_index(t)] for t in range(taps)]
    wide = mix_wide.shape[1] // mix_ref.shape[1]
    mixed = dot(mix_wide, jnp.concatenate(terms[:wide], axis=0))
    for t in range(wide, taps):
        mixed = mixed + dot(mix_ref[t], terms[t])
    return (own.astype(F32) + silu(mixed)).astype(BF16)


def place(acc_ref, at, product, code, rank, cq):
    per = LANES // cq
    slot = lax.rem(rank, per)
    amount = lax.rem((slot - code) * cq + LANES, LANES)
    turned = pltpu.roll(product, amount, axis=1)
    lane = lax.broadcasted_iota(jnp.int32, turned.shape, 1)
    at = at + lax.div(rank, per)
    acc_ref[at] = jnp.where(lax.div(lane, cq) == slot, turned, acc_ref[at])


class Packing:
    def __init__(self, per, cq, channels):
        self.cq, self.channels = cq, channels
        self.lanes = LANES // cq
        self.full, left = divmod(per, self.lanes)
        self.half = 0 < left * 2 <= self.lanes
        if left and not self.half:
            self.full += 1
        self.parts = self.full + self.half
        self.rows = self.full * channels + (channels // 2 if self.half else 0)

    def width(self, tiles):
        return (tiles * self.full + (-(-tiles // 2) if self.half else 0)) * LANES

    def column(self, tiles, hop, rank):
        whole = (hop * self.full * self.lanes + rank) * self.cq
        if not self.half:
            return whole
        split = (
            (tiles * self.full + hop // 2) * LANES
            + hop % 2 * (LANES // 2)
            + (rank - self.full * self.lanes) * self.cq
        )
        return jnp.where(rank < self.full * self.lanes, whole, split)


def cut_kernel(head_ref, tail_ref, first_ref, second_ref):
    right = faces_right()
    head, tail = head_ref[...], tail_ref[...]
    first_ref[...] = jnp.where(right, tail, head)
    second_ref[...] = jnp.where(right, head, tail)


class Level:
    def __init__(self, tables, y_ref, x_ref, mix_ref, restrict_ref, done_ref, acc_ref, counts_ref):
        self.nbr, self.code, self.rcode, self.route = tables
        self.y, self.x, self.mix, self.done, self.acc, self.counts = y_ref, x_ref, mix_ref, done_ref, acc_ref, counts_ref
        self.count, self.channels, self.cells = x_ref.shape
        self.rotations, self.cq = restrict_ref.shape[:2]
        self.taps = mix_ref.shape[0]
        self.blocks = self.route.shape[1]
        self.tiles = self.blocks // self.count
        self.extended = self.count + 2 * RIM
        self.me = lax.axis_index("tile")
        self.mix_wide = joined_mix(mix_ref, min(self.taps, self.cells // self.channels))
        restricts = restrict_ref[...].reshape(self.rotations * self.cq, self.cells)
        self.stacked = jnp.concatenate([restricts] * (LANES // (self.rotations * self.cq)), axis=0)
        for d in range(self.tiles):
            counts_ref[d] = 0

    def y_index(self, b, t):
        local = self.nbr[t, 0, b] - self.me * self.count + RIM
        local = jnp.where(local < 0, local + self.blocks, local)
        local = jnp.where(local >= self.blocks, local - self.blocks, local)
        return self.code[t, 0, b] * self.extended + local

    def pass_over(self, base, store=None):
        for i in range(CHUNK):
            b = base + i
            dest = lax.div(self.route[0, self.me * self.count + b], self.count)
            rank = self.counts[dest]
            self.counts[dest] = rank + 1
            if store is not None:
                store(i, b, dest, rank)

    def run(self, base):
        for i in range(CHUNK):
            b = base + i
            self.done[b] = mixed_skip(
                self.y, functools.partial(self.y_index, b), self.taps, self.mix_wide, self.mix, self.x[b]
            )

    def pack(self, base):
        rows = self.done[base:base + CHUNK].reshape(CHUNK * self.channels, self.cells)
        products = dot_t(rows, self.stacked)
        parts = self.acc.shape[0] // self.tiles

        def store(i, b, dest, rank):
            hop = hop_between(dest, self.me, self.tiles)
            product = products[i * self.channels:(i + 1) * self.channels]
            place(self.acc, hop * parts, product, self.rcode[0, b], rank, self.cq)

        self.pass_over(base, store)


def fetched(sources, targets, sems):
    copies = [
        pltpu.make_async_copy(source, target, sems.at[i])
        for i, (source, target) in enumerate(zip(sources, targets))
    ]
    for copy in copies:
        copy.start()
    return copies


def chunks_of(count):
    return range(0, count, CHUNK)


def is_early(base, count):
    return CHUNK <= base < min((1 + EARLY) * CHUNK, count - CHUNK)


def put_of(done_ref, skip_ref, sems):
    def put(base):
        part = pl.ds(base, CHUNK)
        return pltpu.make_async_copy(done_ref.at[part], skip_ref.at[part], sems.at[base // CHUNK])

    return put


def early_kernel(
    x_ref, table_ref, nbr_ref, code_ref, rcode_ref, route_ref, mix_ref, restrict_ref,
    y_ref, skip_ref, acc_ref,
    nbr, code, rcode, route, mix, restrict, done_ref, counts_ref, in_sems, out_sems,
):
    count, channels, cells = x_ref.shape
    rotations = table_ref.shape[0]
    extended = count + 2 * RIM
    copies = fetched(
        (nbr_ref, code_ref, rcode_ref, route_ref, mix_ref, restrict_ref),
        (nbr, code, rcode, route, mix, restrict), in_sems,
    )
    acc_ref[...] = jnp.zeros(acc_ref.shape, F32)
    for base in chunks_of(count):
        rows = x_ref[base:base + CHUNK].reshape(CHUNK * channels, cells)
        for r in range(rotations):
            product = dot(rows, table_ref[r]).astype(BF16)
            y_ref[pl.ds(r * extended + RIM + base, CHUNK)] = product.reshape(CHUNK, channels, cells)
    for copy in copies:
        copy.wait()
    level = Level((nbr, code, rcode, route), y_ref, x_ref, mix, restrict, done_ref, acc_ref, counts_ref)
    put = put_of(done_ref, skip_ref, out_sems)
    for base in chunks_of(count):
        if is_early(base, count):
            level.run(base)
            put(base).start()
            level.pack(base)
        else:
            level.pass_over(base)
    for base in chunks_of(count):
        if is_early(base, count):
            put(base).wait()


def late_kernel(
    x_ref, table_ref, nbr_ref, code_ref, rcode_ref, route_ref, mix_ref, restrict_ref,
    first_ref, second_ref, y_in_ref, skip_in_ref, acc_in_ref, y_ref, skip_ref, acc_ref, *refs,
):
    sent_refs, refs = refs[:-10], refs[-10:]
    nbr, code, rcode, route, mix, restrict, done_ref, counts_ref, in_sems, out_sems = refs
    del y_in_ref, skip_in_ref, acc_in_ref
    count, channels, cells = x_ref.shape
    rotations = table_ref.shape[0]
    extended = count + 2 * RIM
    copies = fetched(
        (nbr_ref, code_ref, rcode_ref, route_ref, mix_ref, restrict_ref),
        (nbr, code, rcode, route, mix, restrict), in_sems,
    )
    right = faces_right()
    received = [first_ref[...], second_ref[...]]
    before = jnp.where(right, received[1], received[0])
    after = jnp.where(right, received[0], received[1])
    halo = jnp.concatenate([before, after], axis=0).reshape(2 * RIM * channels, cells)
    for r in range(rotations):
        product = dot(halo, table_ref[r]).astype(BF16).reshape(2 * RIM, channels, cells)
        y_ref[r * extended:r * extended + RIM] = product[:RIM]
        y_ref[r * extended + RIM + count:(r + 1) * extended] = product[RIM:]
    for copy in copies:
        copy.wait()
    level = Level((nbr, code, rcode, route), y_ref, x_ref, mix, restrict, done_ref, acc_ref, counts_ref)
    put = put_of(done_ref, skip_ref, out_sems)
    for base in chunks_of(count):
        if is_early(base, count):
            level.pass_over(base)
        else:
            level.run(base)
            put(base).start()
            level.pack(base)
    packing = Packing(count // level.tiles, level.cq, channels)
    half = LANES // 2
    lane = lax.broadcasted_iota(jnp.int32, (channels // 2, LANES), 1)
    for hop in range(level.tiles):
        out = sent_refs[hop]
        at = hop * packing.parts
        for p in range(packing.full):
            out[p * channels:(p + 1) * channels] = acc_ref[at + p].astype(BF16)
        if packing.half:
            value = acc_ref[at + packing.full]
            lower = pltpu.roll(value[channels // 2:], half, axis=1)
            joined = jnp.where(lane < half, value[:channels // 2], lower)
            out[packing.full * channels:] = joined.astype(BF16)
    for base in chunks_of(count):
        if not is_early(base, count):
            put(base).wait()


def order_kernel(count, cq, channels, route_ref, late_ref, order_ref):
    del late_ref
    blocks = route_ref.shape[1]
    tiles = blocks // count
    packing = Packing(count // tiles, cq, channels)
    me = lax.axis_index("tile")
    base = me * count
    route = route_ref[...]
    mine = jnp.where((route >= base) & (route < base + count), 1.0, 0.0)
    shape = (blocks, blocks)
    of, at = (lax.broadcasted_iota(jnp.int32, shape, d) for d in (0, 1))
    earlier = jnp.where((of < at) & (lax.div(of, count) == lax.div(at, count)), 1.0, 0.0)
    rank = dot(jnp.broadcast_to(mine, (8, blocks)).astype(BF16), earlier.astype(BF16))[:1].astype(jnp.int32)
    source = lax.div(lax.broadcasted_iota(jnp.int32, (1, blocks), 1), count)
    hop = hop_between(me, source, tiles)
    column = packing.column(tiles, hop, rank).astype(F32)
    cells = count * cq
    cell = lax.broadcasted_iota(jnp.int32, (cells, blocks), 0)
    found = jnp.where(route == base + lax.div(cell, cq), column, 0.0)
    wanted = jnp.sum(found, axis=1, keepdims=True)
    wanted = wanted + lax.rem(lax.broadcasted_iota(jnp.int32, (cells, 1), 0), cq).astype(F32)
    across = jnp.transpose(jnp.broadcast_to(wanted, (cells, LANES)))[:1].astype(jnp.int32)
    step = LANES
    for row in range(0, order_ref.shape[0], step):
        index = row + lax.broadcasted_iota(jnp.int32, (step, cells), 0)
        order_ref[row:row + step] = jnp.where(index == across, 1.0, 0.0).astype(BF16)


def merge_kernel(per, cq, order_ref, *refs):
    arrived, (coarse_ref, first_ref, second_ref) = refs[:-3], refs[-3:]
    order = hop_order(len(arrived))
    arrived = [arrived[0]] + [arrived[1 + order.index(hop)] for hop in range(1, len(arrived))]
    blocks, channels, cells = coarse_ref.shape
    tiles = len(arrived)
    packing = Packing(per, cq, channels)
    columns = [ref[p * channels:(p + 1) * channels] for ref in arrived for p in range(packing.full)]
    if packing.half:
        half = LANES // 2
        lane = lax.broadcasted_iota(jnp.int32, (channels // 2, LANES), 1)
        halves = [ref[packing.full * channels:].astype(F32) for ref in arrived]
        halves += [jnp.zeros_like(halves[0])] * (tiles % 2)
        for one, other in zip(halves[::2], halves[1::2]):
            upper = jnp.where(lane < half, one, pltpu.roll(other, half, axis=1))
            lower = jnp.where(lane < half, pltpu.roll(one, half, axis=1), other)
            columns.append(jnp.concatenate([upper, lower], axis=0).astype(BF16))
    joined = jnp.concatenate(columns, axis=1)
    values = [
        dot(joined, order_ref[:, c * cells:(c + 1) * cells]).astype(BF16) for c in range(blocks)
    ]
    for c in range(blocks):
        coarse_ref[c] = values[c]
    right = faces_right()
    first_ref[...] = jnp.where(right, values[-1], values[0])
    second_ref[...] = jnp.where(right, values[0], values[-1])


def inside_kernel(code_ref, coarse_ref, spatial_ref, mix_ref, total_ref, table_ref):
    blocks = coarse_ref.shape[0]
    values = [coarse_ref[c] for c in range(blocks)]
    for c in range(blocks):
        total = dot(mix_ref[0], values[c])
        for e, other in enumerate((c - 1, c + 1)):
            if 0 <= other < blocks:
                edge = dot(values[other], spatial_ref[code_ref[c, 0, e]]).astype(BF16)
                total = total + dot(mix_ref[e + 1], edge)
        total_ref[c] = total
        table_ref[2 + c] = spatial_ref[code_ref[c, 0, 2]]
    table_ref[0] = spatial_ref[code_ref[0, 0, 0]]
    table_ref[1] = spatial_ref[code_ref[blocks - 1, 0, 1]]


def coarse_kernel(seam_ref, first_ref, second_ref, coarse_ref, total_ref, table_ref, mix_ref, out_ref):
    blocks = coarse_ref.shape[0]
    right = faces_right()
    left_rows = jnp.where(right, second_ref[...], first_ref[...])
    right_rows = jnp.where(right, first_ref[...], second_ref[...])
    left_edge = dot(left_rows, table_ref[0]).astype(BF16)
    right_edge = dot(right_rows, table_ref[1]).astype(BF16)
    for c in range(blocks):
        total = total_ref[c] + dot(mix_ref[3], dot(seam_ref[c], table_ref[2 + c]).astype(BF16))
        if c == 0:
            total = total + dot(mix_ref[1], left_edge)
        if c == blocks - 1:
            total = total + dot(mix_ref[2], right_edge)
        out_ref[c] = (coarse_ref[c].astype(F32) + silu(total)).astype(BF16)


def params(mib=VMEM_MIB):
    return pltpu.CompilerParams(vmem_limit_bytes=mib * 1024 * 1024)


def per_device(
    fine, conv_spatial, conv_mix, neighbours, fine_codes, restrict, restrict_codes, route,
    coarse_spatial, coarse_mix, coarse_codes,
):
    x = fine[0, 0]
    count, channels, cells = x.shape
    rotations = conv_spatial.shape[0]
    cq = restrict.shape[2]
    tiles = route.shape[1] // count
    per = count // tiles
    blocks = count * cq // cells
    packing = Packing(per, cq, channels)
    nbr, codes = neighbours.transpose(2, 0, 1), fine_codes.transpose(2, 0, 1)
    narrow = restrict.transpose(0, 2, 1)

    rim_shape = jax.ShapeDtypeStruct((RIM, channels, cells), BF16)
    first, second = pl.pallas_call(
        cut_kernel,
        out_shape=(rim_shape, rim_shape),
        in_specs=[VMEM()] * 2,
        out_specs=(VMEM(),) * 2,
        compiler_params=params(),
        cost_estimate=pl.CostEstimate(flops=4 * 10**9, bytes_accessed=10**6, transcendentals=0),
        name="cut",
    )(x[:RIM], x[count - RIM:])
    second = swapped(False, second, "tile")
    first = swapped(True, first, "tile")

    y_shape = (rotations * (count + 2 * RIM), channels, cells)
    steps = count // CHUNK
    tables = (nbr, codes, restrict_codes, route)
    shared = [pltpu.SMEM(a.shape, jnp.int32) for a in tables] + [
        pltpu.VMEM(conv_mix.shape, BF16),
        pltpu.VMEM(narrow.shape, BF16),
        pltpu.VMEM(x.shape, BF16),
        pltpu.SMEM((tiles,), jnp.int32),
        pltpu.SemaphoreType.DMA((6,)),
        pltpu.SemaphoreType.DMA((steps,)),
    ]
    made = (
        jax.ShapeDtypeStruct(y_shape, BF16),
        jax.ShapeDtypeStruct(x.shape, BF16),
        jax.ShapeDtypeStruct((tiles * packing.parts, channels, LANES), F32),
    )
    given = (x, conv_spatial) + tables + (conv_mix, narrow)
    given_specs = [VMEM()] * 2 + [ANY()] * 6
    y, skip, acc = pl.pallas_call(
        early_kernel,
        out_shape=made,
        in_specs=given_specs,
        out_specs=(VMEM(), ANY(), VMEM()),
        scratch_shapes=shared,
        compiler_params=params(),
        cost_estimate=pl.CostEstimate(flops=4 * 10**9, bytes_accessed=4 * 10**6, transcendentals=10**6),
        name="early",
    )(*given)

    sent_shape = jax.ShapeDtypeStruct((packing.rows, LANES), BF16)
    _, skip, _, *sent = pl.pallas_call(
        late_kernel,
        out_shape=made + (sent_shape,) * tiles,
        in_specs=given_specs + [VMEM()] * 3 + [ANY(), VMEM()],
        out_specs=(VMEM(), ANY(), VMEM()) + (VMEM(),) * tiles,
        scratch_shapes=shared,
        input_output_aliases={10: 0, 11: 1, 12: 2},
        compiler_params=params(),
        name="late",
    )(*given, first, second, y, skip, acc)

    order = pl.pallas_call(
        functools.partial(order_kernel, count, cq, channels),
        out_shape=jax.ShapeDtypeStruct((packing.width(tiles), count * cq), BF16),
        in_specs=[VMEM(), VMEM()],
        out_specs=VMEM(),
        compiler_params=params(),
        name="order",
    )(route, sent[0])
    arrived = [sent[0]] + [exchanged(sent[hop], "tile", hop) for hop in range(1, tiles)]

    block_shape = jax.ShapeDtypeStruct((channels, cells), BF16)
    coarse, first, second = pl.pallas_call(
        functools.partial(merge_kernel, per, cq),
        out_shape=(jax.ShapeDtypeStruct((blocks, channels, cells), BF16), block_shape, block_shape),
        in_specs=[VMEM()] * (1 + tiles),
        out_specs=(VMEM(), VMEM(), VMEM()),
        compiler_params=params(),
        name="merge",
    )(order, arrived[0], *[arrived[hop] for hop in hop_order(tiles)])

    second = swapped(False, second, "tile")
    first = swapped(True, first, "tile")
    seam = shifted(coarse, "sect", 1)
    total, tables = pl.pallas_call(
        inside_kernel,
        out_shape=(
            jax.ShapeDtypeStruct(coarse.shape, F32),
            jax.ShapeDtypeStruct((2 + blocks,) + coarse_spatial.shape[1:], BF16),
        ),
        in_specs=[SMEM()] + [VMEM()] * 3,
        out_specs=(VMEM(), VMEM()),
        compiler_params=params(),
        name="inside",
    )(coarse_codes.transpose(1, 0, 2), coarse, coarse_spatial, coarse_mix)
    coarse_out = pl.pallas_call(
        coarse_kernel,
        out_shape=jax.ShapeDtypeStruct(coarse.shape, BF16),
        in_specs=[VMEM()] * 7,
        out_specs=VMEM(),
        compiler_params=params(),
        name="coarse",
    )(seam, first, second, coarse, total, tables, coarse_mix)
    return (skip[None, None], coarse_out[None, None])


def solution(mesh):
    data = P(("groups", "chan"), "sect", "tile", None, None)
    placed = (
        data,
        P(),
        P(),
        P("sect", "tile", None),
        P("sect", "tile", None),
        P(),
        P("sect", "tile"),
        P("sect", None),
        P(),
        P(),
        P("sect", "tile", None),
    )
    return jax.shard_map(
        per_device, mesh=mesh, in_specs=placed, out_specs=(data, data), check_vma=False
    )
```

```python
import functools

import jax
import jax.numpy as jnp
from jax import lax
from jax.experimental import pallas as pl
from jax.experimental.pallas import tpu as pltpu
from jax.sharding import PartitionSpec as P

LANES = 128
RIM = 2
CHUNK = 8
EARLY = 4
VMEM_MIB = 40

SMEM = functools.partial(pl.BlockSpec, memory_space=pltpu.SMEM)
VMEM = functools.partial(pl.BlockSpec, memory_space=pltpu.VMEM)
ANY = functools.partial(pl.BlockSpec, memory_space=pl.ANY)
HBM = functools.partial(pl.BlockSpec, memory_space=pltpu.HBM)
F32 = jnp.float32
BF16 = jnp.bfloat16


def dot(a, b):
    return jnp.dot(a, b, preferred_element_type=F32)


def silu(v):
    return v * (0.5 + 0.5 * jnp.tanh(0.5 * v))


def shifted(value, axis, steps):
    count = lax.axis_size(axis)
    return lax.ppermute(value, axis, [(i, (i + steps) % count) for i in range(count)])


def joined_mix(mix_ref, terms):
    return jnp.concatenate([mix_ref[t] for t in range(terms)], axis=1)


def dot_t(a, b):
    return lax.dot_general(a, b, (((1,), (1,)), ((), ())), preferred_element_type=F32)


def swapped(even, value, axis):
    count = lax.axis_size(axis)
    first = 0 if even else 1
    pairs = []
    for i in range(first, count + first, 2):
        here, there = i % count, (i + 1) % count
        pairs += [(here, there), (there, here)]
    return lax.ppermute(value, axis, pairs)


def paired(tiles):
    return tiles & (tiles - 1) == 0


def hop_between(dest, source, tiles):
    if paired(tiles):
        return lax.bitwise_xor(dest, source)
    return lax.rem(dest - source + tiles, tiles)


def exchanged(value, axis, hop):
    count = lax.axis_size(axis)
    pairs = [(i, i ^ hop if paired(count) else (i + hop) % count) for i in range(count)]
    return lax.ppermute(value, axis, pairs)


def hop_order(tiles):
    return list(range(tiles // 2, tiles)) + list(range(1, tiles // 2))


def faces_right():
    return lax.rem(lax.axis_index("tile"), 2) == 0


def mixed_skip(y_ref, y_index, taps, mix_wide, mix_ref, own):
    terms = [y_ref[y_index(t)] for t in range(taps)]
    wide = mix_wide.shape[1] // mix_ref.shape[1]
    mixed = dot(mix_wide, jnp.concatenate(terms[:wide], axis=0))
    for t in range(wide, taps):
        mixed = mixed + dot(mix_ref[t], terms[t])
    return (own.astype(F32) + silu(mixed)).astype(BF16)


def place(acc_ref, at, product, code, rank, cq):
    per = LANES // cq
    slot = lax.rem(rank, per)
    amount = lax.rem((slot - code) * cq + LANES, LANES)
    turned = pltpu.roll(product, amount, axis=1)
    lane = lax.broadcasted_iota(jnp.int32, turned.shape, 1)
    at = at + lax.div(rank, per)
    acc_ref[at] = jnp.where(lax.div(lane, cq) == slot, turned, acc_ref[at])


class Packing:
    def __init__(self, per, cq, channels):
        self.cq, self.channels = cq, channels
        self.lanes = LANES // cq
        self.full, left = divmod(per, self.lanes)
        self.half = 0 < left * 2 <= self.lanes
        if left and not self.half:
            self.full += 1
        self.parts = self.full + self.half
        self.rows = self.full * channels + (channels // 2 if self.half else 0)

    def width(self, tiles):
        return (tiles * self.full + (-(-tiles // 2) if self.half else 0)) * LANES

    def column(self, tiles, hop, rank):
        whole = (hop * self.full * self.lanes + rank) * self.cq
        if not self.half:
            return whole
        split = (
            (tiles * self.full + hop // 2) * LANES
            + hop % 2 * (LANES // 2)
            + (rank - self.full * self.lanes) * self.cq
        )
        return jnp.where(rank < self.full * self.lanes, whole, split)


def cut_kernel(head_ref, tail_ref, first_ref, second_ref):
    right = faces_right()
    head, tail = head_ref[...], tail_ref[...]
    first_ref[...] = jnp.where(right, tail, head)
    second_ref[...] = jnp.where(right, head, tail)


class Level:
    def __init__(self, tables, y_ref, x_ref, mix_ref, restrict_ref, done_ref, acc_ref, counts_ref):
        self.nbr, self.code, self.rcode, self.route = tables
        self.y, self.x, self.mix, self.done, self.acc, self.counts = y_ref, x_ref, mix_ref, done_ref, acc_ref, counts_ref
        self.count, self.channels, self.cells = x_ref.shape
        self.rotations, self.cq = restrict_ref.shape[:2]
        self.taps = mix_ref.shape[0]
        self.blocks = self.route.shape[1]
        self.tiles = self.blocks // self.count
        self.extended = self.count + 2 * RIM
        self.me = lax.axis_index("tile")
        self.mix_wide = joined_mix(mix_ref, min(self.taps, self.cells // self.channels))
        restricts = restrict_ref[...].reshape(self.rotations * self.cq, self.cells)
        self.stacked = jnp.concatenate([restricts] * (LANES // (self.rotations * self.cq)), axis=0)
        for d in range(self.tiles):
            counts_ref[d] = 0

    def y_index(self, b, t):
        local = self.nbr[t, 0, b] - self.me * self.count + RIM
        local = jnp.where(local < 0, local + self.blocks, local)
        local = jnp.where(local >= self.blocks, local - self.blocks, local)
        return self.code[t, 0, b] * self.extended + local

    def pass_over(self, base, store=None):
        for i in range(CHUNK):
            b = base + i
            dest = lax.div(self.route[0, self.me * self.count + b], self.count)
            rank = self.counts[dest]
            self.counts[dest] = rank + 1
            if store is not None:
                store(i, b, dest, rank)

    def run(self, base):
        for i in range(CHUNK):
            b = base + i
            self.done[b] = mixed_skip(
                self.y, functools.partial(self.y_index, b), self.taps, self.mix_wide, self.mix, self.x[b]
            )

    def pack(self, base):
        rows = self.done[base:base + CHUNK].reshape(CHUNK * self.channels, self.cells)
        products = dot_t(rows, self.stacked)
        parts = self.acc.shape[0] // self.tiles

        def store(i, b, dest, rank):
            hop = hop_between(dest, self.me, self.tiles)
            product = products[i * self.channels:(i + 1) * self.channels]
            place(self.acc, hop * parts, product, self.rcode[0, b], rank, self.cq)

        self.pass_over(base, store)


def fetched(sources, targets, sems):
    copies = [
        pltpu.make_async_copy(source, target, sems.at[i])
        for i, (source, target) in enumerate(zip(sources, targets))
    ]
    for copy in copies:
        copy.start()
    return copies


def chunks_of(count):
    return range(0, count, CHUNK)


def is_early(base, count):
    return CHUNK <= base < min((1 + EARLY) * CHUNK, count - CHUNK)


def early_kernel(
    x_ref, table_ref, nbr_ref, code_ref, rcode_ref, route_ref, mix_ref, restrict_ref,
    y_ref, done_ref, acc_ref,
    nbr, code, rcode, route, mix, restrict, counts_ref, in_sems,
):
    count, channels, cells = x_ref.shape
    rotations = table_ref.shape[0]
    extended = count + 2 * RIM
    copies = fetched(
        (nbr_ref, code_ref, rcode_ref, route_ref, mix_ref, restrict_ref),
        (nbr, code, rcode, route, mix, restrict), in_sems,
    )
    acc_ref[...] = jnp.zeros(acc_ref.shape, F32)
    for base in chunks_of(count):
        rows = x_ref[base:base + CHUNK].reshape(CHUNK * channels, cells)
        for r in range(rotations):
            product = dot(rows, table_ref[r]).astype(BF16)
            y_ref[pl.ds(r * extended + RIM + base, CHUNK)] = product.reshape(CHUNK, channels, cells)
    for copy in copies:
        copy.wait()
    level = Level((nbr, code, rcode, route), y_ref, x_ref, mix, restrict, done_ref, acc_ref, counts_ref)
    for base in chunks_of(count):
        if is_early(base, count):
            level.run(base)
            level.pack(base)
        else:
            level.pass_over(base)


def late_kernel(
    x_ref, table_ref, nbr_ref, code_ref, rcode_ref, route_ref, mix_ref, restrict_ref,
    first_ref, second_ref, y_in_ref, done_in_ref, acc_in_ref, y_ref, done_ref, acc_ref, *refs,
):
    sent_refs, refs = refs[:-8], refs[-8:]
    nbr, code, rcode, route, mix, restrict, counts_ref, in_sems = refs
    del y_in_ref, done_in_ref, acc_in_ref
    count, channels, cells = x_ref.shape
    rotations = table_ref.shape[0]
    extended = count + 2 * RIM
    copies = fetched(
        (nbr_ref, code_ref, rcode_ref, route_ref, mix_ref, restrict_ref),
        (nbr, code, rcode, route, mix, restrict), in_sems,
    )
    right = faces_right()
    received = [first_ref[...], second_ref[...]]
    before = jnp.where(right, received[1], received[0])
    after = jnp.where(right, received[0], received[1])
    halo = jnp.concatenate([before, after], axis=0).reshape(2 * RIM * channels, cells)
    for r in range(rotations):
        product = dot(halo, table_ref[r]).astype(BF16).reshape(2 * RIM, channels, cells)
        y_ref[r * extended:r * extended + RIM] = product[:RIM]
        y_ref[r * extended + RIM + count:(r + 1) * extended] = product[RIM:]
    for copy in copies:
        copy.wait()
    level = Level((nbr, code, rcode, route), y_ref, x_ref, mix, restrict, done_ref, acc_ref, counts_ref)
    for base in chunks_of(count):
        if is_early(base, count):
            level.pass_over(base)
        else:
            level.run(base)
            level.pack(base)
    packing = Packing(count // level.tiles, level.cq, channels)
    half = LANES // 2
    lane = lax.broadcasted_iota(jnp.int32, (channels // 2, LANES), 1)
    for hop in range(level.tiles):
        out = sent_refs[hop]
        at = hop * packing.parts
        for p in range(packing.full):
            out[p * channels:(p + 1) * channels] = acc_ref[at + p].astype(BF16)
        if packing.half:
            value = acc_ref[at + packing.full]
            lower = pltpu.roll(value[channels // 2:], half, axis=1)
            joined = jnp.where(lane < half, value[:channels // 2], lower)
            out[packing.full * channels:] = joined.astype(BF16)


def order_kernel(cq, route_ref, done_ref, order_ref, skip_ref, sems):
    count, channels = done_ref.shape[:2]
    copies = [
        pltpu.make_async_copy(
            done_ref.at[pl.ds(base, CHUNK)], skip_ref.at[pl.ds(base, CHUNK)], sems.at[base // CHUNK]
        )
        for base in chunks_of(count)
    ]
    for copy in copies:
        copy.start()
    blocks = route_ref.shape[1]
    tiles = blocks // count
    packing = Packing(count // tiles, cq, channels)
    me = lax.axis_index("tile")
    base = me * count
    route = route_ref[...]
    mine = jnp.where((route >= base) & (route < base + count), 1.0, 0.0)
    shape = (blocks, blocks)
    of, at = (lax.broadcasted_iota(jnp.int32, shape, d) for d in (0, 1))
    earlier = jnp.where((of < at) & (lax.div(of, count) == lax.div(at, count)), 1.0, 0.0)
    rank = dot(jnp.broadcast_to(mine, (8, blocks)).astype(BF16), earlier.astype(BF16))[:1].astype(jnp.int32)
    source = lax.div(lax.broadcasted_iota(jnp.int32, (1, blocks), 1), count)
    hop = hop_between(me, source, tiles)
    column = packing.column(tiles, hop, rank).astype(F32)
    cells = count * cq
    cell = lax.broadcasted_iota(jnp.int32, (cells, blocks), 0)
    found = jnp.where(route == base + lax.div(cell, cq), column, 0.0)
    wanted = jnp.sum(found, axis=1, keepdims=True)
    wanted = wanted + lax.rem(lax.broadcasted_iota(jnp.int32, (cells, 1), 0), cq).astype(F32)
    across = jnp.transpose(jnp.broadcast_to(wanted, (cells, LANES)))[:1].astype(jnp.int32)
    step = LANES
    for row in range(0, order_ref.shape[0], step):
        index = row + lax.broadcasted_iota(jnp.int32, (step, cells), 0)
        order_ref[row:row + step] = jnp.where(index == across, 1.0, 0.0).astype(BF16)
    for copy in copies:
        copy.wait()


def merge_kernel(per, cq, order_ref, *refs):
    arrived, (coarse_ref, first_ref, second_ref) = refs[:-3], refs[-3:]
    order = hop_order(len(arrived))
    arrived = [arrived[0]] + [arrived[1 + order.index(hop)] for hop in range(1, len(arrived))]
    blocks, channels, cells = coarse_ref.shape
    tiles = len(arrived)
    packing = Packing(per, cq, channels)
    columns = [ref[p * channels:(p + 1) * channels] for ref in arrived for p in range(packing.full)]
    if packing.half:
        half = LANES // 2
        lane = lax.broadcasted_iota(jnp.int32, (channels // 2, LANES), 1)
        halves = [ref[packing.full * channels:].astype(F32) for ref in arrived]
        halves += [jnp.zeros_like(halves[0])] * (tiles % 2)
        for one, other in zip(halves[::2], halves[1::2]):
            upper = jnp.where(lane < half, one, pltpu.roll(other, half, axis=1))
            lower = jnp.where(lane < half, pltpu.roll(one, half, axis=1), other)
            columns.append(jnp.concatenate([upper, lower], axis=0).astype(BF16))
    joined = jnp.concatenate(columns, axis=1)
    values = [
        dot(joined, order_ref[:, c * cells:(c + 1) * cells]).astype(BF16) for c in range(blocks)
    ]
    for c in range(blocks):
        coarse_ref[c] = values[c]
    right = faces_right()
    first_ref[...] = jnp.where(right, values[-1], values[0])
    second_ref[...] = jnp.where(right, values[0], values[-1])


def inside_kernel(code_ref, coarse_ref, spatial_ref, mix_ref, total_ref, table_ref):
    blocks = coarse_ref.shape[0]
    values = [coarse_ref[c] for c in range(blocks)]
    for c in range(blocks):
        total = dot(mix_ref[0], values[c])
        for e, other in enumerate((c - 1, c + 1)):
            if 0 <= other < blocks:
                edge = dot(values[other], spatial_ref[code_ref[c, 0, e]]).astype(BF16)
                total = total + dot(mix_ref[e + 1], edge)
        total_ref[c] = total
        table_ref[2 + c] = spatial_ref[code_ref[c, 0, 2]]
    table_ref[0] = spatial_ref[code_ref[0, 0, 0]]
    table_ref[1] = spatial_ref[code_ref[blocks - 1, 0, 1]]


def coarse_kernel(seam_ref, first_ref, second_ref, coarse_ref, total_ref, table_ref, mix_ref, out_ref):
    blocks = coarse_ref.shape[0]
    right = faces_right()
    left_rows = jnp.where(right, second_ref[...], first_ref[...])
    right_rows = jnp.where(right, first_ref[...], second_ref[...])
    left_edge = dot(left_rows, table_ref[0]).astype(BF16)
    right_edge = dot(right_rows, table_ref[1]).astype(BF16)
    for c in range(blocks):
        total = total_ref[c] + dot(mix_ref[3], dot(seam_ref[c], table_ref[2 + c]).astype(BF16))
        if c == 0:
            total = total + dot(mix_ref[1], left_edge)
        if c == blocks - 1:
            total = total + dot(mix_ref[2], right_edge)
        out_ref[c] = (coarse_ref[c].astype(F32) + silu(total)).astype(BF16)


def params(mib=VMEM_MIB):
    return pltpu.CompilerParams(vmem_limit_bytes=mib * 1024 * 1024)


def per_device(
    fine, conv_spatial, conv_mix, neighbours, fine_codes, restrict, restrict_codes, route,
    coarse_spatial, coarse_mix, coarse_codes,
):
    x = fine[0, 0]
    count, channels, cells = x.shape
    rotations = conv_spatial.shape[0]
    cq = restrict.shape[2]
    tiles = route.shape[1] // count
    per = count // tiles
    blocks = count * cq // cells
    packing = Packing(per, cq, channels)
    nbr, codes = neighbours.transpose(2, 0, 1), fine_codes.transpose(2, 0, 1)
    narrow = restrict.transpose(0, 2, 1)

    rim_shape = jax.ShapeDtypeStruct((RIM, channels, cells), BF16)
    first, second = pl.pallas_call(
        cut_kernel,
        out_shape=(rim_shape, rim_shape),
        in_specs=[VMEM()] * 2,
        out_specs=(VMEM(),) * 2,
        compiler_params=params(),
        cost_estimate=pl.CostEstimate(flops=4 * 10**9, bytes_accessed=10**6, transcendentals=0),
        name="cut",
    )(x[:RIM], x[count - RIM:])
    second = swapped(False, second, "tile")
    first = swapped(True, first, "tile")

    y_shape = (rotations * (count + 2 * RIM), channels, cells)
    steps = count // CHUNK
    tables = (nbr, codes, restrict_codes, route)
    shared = [pltpu.SMEM(a.shape, jnp.int32) for a in tables] + [
        pltpu.VMEM(conv_mix.shape, BF16),
        pltpu.VMEM(narrow.shape, BF16),
        pltpu.SMEM((tiles,), jnp.int32),
        pltpu.SemaphoreType.DMA((6,)),
    ]
    made = (
        jax.ShapeDtypeStruct(y_shape, BF16),
        jax.ShapeDtypeStruct(x.shape, BF16),
        jax.ShapeDtypeStruct((tiles * packing.parts, channels, LANES), F32),
    )
    given = (x, conv_spatial) + tables + (conv_mix, narrow)
    given_specs = [VMEM()] * 2 + [ANY()] * 6
    y, done, acc = pl.pallas_call(
        early_kernel,
        out_shape=made,
        in_specs=given_specs,
        out_specs=(VMEM(), VMEM(), VMEM()),
        scratch_shapes=shared,
        compiler_params=params(),
        cost_estimate=pl.CostEstimate(flops=4 * 10**9, bytes_accessed=4 * 10**6, transcendentals=10**6),
        name="early",
    )(*given)

    sent_shape = jax.ShapeDtypeStruct((packing.rows, LANES), BF16)
    _, done, _, *sent = pl.pallas_call(
        late_kernel,
        out_shape=made + (sent_shape,) * tiles,
        in_specs=given_specs + [VMEM()] * 5,
        out_specs=(VMEM(),) * (3 + tiles),
        scratch_shapes=shared,
        input_output_aliases={10: 0, 11: 1, 12: 2},
        compiler_params=params(),
        name="late",
    )(*given, first, second, y, done, acc)

    order, skip = pl.pallas_call(
        functools.partial(order_kernel, cq),
        out_shape=(
            jax.ShapeDtypeStruct((packing.width(tiles), count * cq), BF16),
            jax.ShapeDtypeStruct(x.shape, BF16),
        ),
        in_specs=[VMEM(), VMEM()],
        out_specs=(VMEM(), ANY()),
        scratch_shapes=[pltpu.SemaphoreType.DMA((steps,))],
        compiler_params=params(),
        name="order",
    )(route, done)
    arrived = [sent[0]] + [exchanged(sent[hop], "tile", hop) for hop in range(1, tiles)]

    block_shape = jax.ShapeDtypeStruct((channels, cells), BF16)
    coarse, first, second = pl.pallas_call(
        functools.partial(merge_kernel, per, cq),
        out_shape=(jax.ShapeDtypeStruct((blocks, channels, cells), BF16), block_shape, block_shape),
        in_specs=[VMEM()] * (1 + tiles),
        out_specs=(VMEM(), VMEM(), VMEM()),
        compiler_params=params(),
        name="merge",
    )(order, arrived[0], *[arrived[hop] for hop in hop_order(tiles)])

    second = swapped(False, second, "tile")
    first = swapped(True, first, "tile")
    seam = shifted(coarse, "sect", 1)
    total, tables = pl.pallas_call(
        inside_kernel,
        out_shape=(
            jax.ShapeDtypeStruct(coarse.shape, F32),
            jax.ShapeDtypeStruct((2 + blocks,) + coarse_spatial.shape[1:], BF16),
        ),
        in_specs=[SMEM()] + [VMEM()] * 3,
        out_specs=(VMEM(), VMEM()),
        compiler_params=params(),
        name="inside",
    )(coarse_codes.transpose(1, 0, 2), coarse, coarse_spatial, coarse_mix)
    coarse_out = pl.pallas_call(
        coarse_kernel,
        out_shape=jax.ShapeDtypeStruct(coarse.shape, BF16),
        in_specs=[VMEM()] * 7,
        out_specs=VMEM(),
        compiler_params=params(),
        name="coarse",
    )(seam, first, second, coarse, total, tables, coarse_mix)
    return (skip[None, None], coarse_out[None, None])


def solution(mesh):
    data = P(("groups", "chan"), "sect", "tile", None, None)
    placed = (
        data,
        P(),
        P(),
        P("sect", "tile", None),
        P("sect", "tile", None),
        P(),
        P("sect", "tile"),
        P("sect", None),
        P(),
        P(),
        P("sect", "tile", None),
    )
    return jax.shard_map(
        per_device, mesh=mesh, in_specs=placed, out_specs=(data, data), check_vma=False
    )
```

```python
import functools

import jax
import jax.numpy as jnp
from jax import lax
from jax.experimental import pallas as pl
from jax.experimental.pallas import tpu as pltpu
from jax.sharding import PartitionSpec as P

LANES = 128
RIM = 2
CHUNK = 8
EARLY = 4
VMEM_MIB = 40

SMEM = functools.partial(pl.BlockSpec, memory_space=pltpu.SMEM)
VMEM = functools.partial(pl.BlockSpec, memory_space=pltpu.VMEM)
ANY = functools.partial(pl.BlockSpec, memory_space=pl.ANY)
HBM = functools.partial(pl.BlockSpec, memory_space=pltpu.HBM)
F32 = jnp.float32
BF16 = jnp.bfloat16


def dot(a, b):
    return jnp.dot(a, b, preferred_element_type=F32)


def silu(v):
    return v * (0.5 + 0.5 * jnp.tanh(0.5 * v))


def shifted(value, axis, steps):
    count = lax.axis_size(axis)
    return lax.ppermute(value, axis, [(i, (i + steps) % count) for i in range(count)])


def joined_mix(mix_ref, terms):
    return jnp.concatenate([mix_ref[t] for t in range(terms)], axis=1)


def dot_t(a, b):
    return lax.dot_general(a, b, (((1,), (1,)), ((), ())), preferred_element_type=F32)


def swapped(even, value, axis):
    count = lax.axis_size(axis)
    first = 0 if even else 1
    pairs = []
    for i in range(first, count + first, 2):
        here, there = i % count, (i + 1) % count
        pairs += [(here, there), (there, here)]
    return lax.ppermute(value, axis, pairs)


def paired(tiles):
    return tiles & (tiles - 1) == 0


def hop_between(dest, source, tiles):
    if paired(tiles):
        return lax.bitwise_xor(dest, source)
    return lax.rem(dest - source + tiles, tiles)


def exchanged(value, axis, hop):
    count = lax.axis_size(axis)
    pairs = [(i, i ^ hop if paired(count) else (i + hop) % count) for i in range(count)]
    return lax.ppermute(value, axis, pairs)


def hop_order(tiles):
    return list(range(tiles // 2, tiles)) + list(range(1, tiles // 2))


def faces_right():
    return lax.rem(lax.axis_index("tile"), 2) == 0


def mixed_skip(y_ref, y_index, taps, mix_wide, mix_ref, own):
    terms = [y_ref[y_index(t)] for t in range(taps)]
    wide = mix_wide.shape[1] // mix_ref.shape[1]
    mixed = dot(mix_wide, jnp.concatenate(terms[:wide], axis=0))
    for t in range(wide, taps):
        mixed = mixed + dot(mix_ref[t], terms[t])
    return (own.astype(F32) + silu(mixed)).astype(BF16)


def place(acc_ref, at, product, code, rank, cq):
    per = LANES // cq
    slot = lax.rem(rank, per)
    amount = lax.rem((slot - code) * cq + LANES, LANES)
    turned = pltpu.roll(product, amount, axis=1)
    lane = lax.broadcasted_iota(jnp.int32, turned.shape, 1)
    at = at + lax.div(rank, per)
    acc_ref[at] = jnp.where(lax.div(lane, cq) == slot, turned, acc_ref[at])


class Packing:
    def __init__(self, per, cq, channels):
        self.cq, self.channels = cq, channels
        self.lanes = LANES // cq
        self.full, left = divmod(per, self.lanes)
        self.half = 0 < left * 2 <= self.lanes
        if left and not self.half:
            self.full += 1
        self.parts = self.full + self.half
        self.rows = self.full * channels + (channels // 2 if self.half else 0)

    def width(self, tiles):
        return (tiles * self.full + (-(-tiles // 2) if self.half else 0)) * LANES

    def column(self, tiles, hop, rank):
        whole = (hop * self.full * self.lanes + rank) * self.cq
        if not self.half:
            return whole
        split = (
            (tiles * self.full + hop // 2) * LANES
            + hop % 2 * (LANES // 2)
            + (rank - self.full * self.lanes) * self.cq
        )
        return jnp.where(rank < self.full * self.lanes, whole, split)


def cut_kernel(head_ref, tail_ref, first_ref, second_ref):
    right = faces_right()
    head, tail = head_ref[...], tail_ref[...]
    first_ref[...] = jnp.where(right, tail, head)
    second_ref[...] = jnp.where(right, head, tail)


class Level:
    def __init__(self, tables, y_ref, x_ref, mix_ref, restrict_ref, done_ref, acc_ref, counts_ref):
        self.nbr, self.code, self.rcode, self.route = tables
        self.y, self.x, self.mix, self.done, self.acc, self.counts = y_ref, x_ref, mix_ref, done_ref, acc_ref, counts_ref
        self.count, self.channels, self.cells = x_ref.shape
        self.rotations, self.cq = restrict_ref.shape[:2]
        self.taps = mix_ref.shape[0]
        self.blocks = self.route.shape[1]
        self.tiles = self.blocks // self.count
        self.extended = self.count + 2 * RIM
        self.me = lax.axis_index("tile")
        self.mix_wide = joined_mix(mix_ref, min(self.taps, self.cells // self.channels))
        restricts = restrict_ref[...].reshape(self.rotations * self.cq, self.cells)
        self.stacked = jnp.concatenate([restricts] * (LANES // (self.rotations * self.cq)), axis=0)
        for d in range(self.tiles):
            counts_ref[d] = 0

    def y_index(self, b, t):
        local = self.nbr[t, 0, b] - self.me * self.count + RIM
        local = jnp.where(local < 0, local + self.blocks, local)
        local = jnp.where(local >= self.blocks, local - self.blocks, local)
        return self.code[t, 0, b] * self.extended + local

    def pass_over(self, base, store=None):
        for i in range(CHUNK):
            b = base + i
            dest = lax.div(self.route[0, self.me * self.count + b], self.count)
            rank = self.counts[dest]
            self.counts[dest] = rank + 1
            if store is not None:
                store(i, b, dest, rank)

    def run(self, base):
        for i in range(CHUNK):
            b = base + i
            self.done[b] = mixed_skip(
                self.y, functools.partial(self.y_index, b), self.taps, self.mix_wide, self.mix, self.x[b]
            )

    def pack(self, base):
        rows = self.done[base:base + CHUNK].reshape(CHUNK * self.channels, self.cells)
        products = dot_t(rows, self.stacked)
        parts = self.acc.shape[0] // self.tiles

        def store(i, b, dest, rank):
            hop = hop_between(dest, self.me, self.tiles)
            product = products[i * self.channels:(i + 1) * self.channels]
            place(self.acc, hop * parts, product, self.rcode[0, b], rank, self.cq)

        self.pass_over(base, store)


def fetched(sources, targets, sems):
    copies = [
        pltpu.make_async_copy(source, target, sems.at[i])
        for i, (source, target) in enumerate(zip(sources, targets))
    ]
    for copy in copies:
        copy.start()
    return copies


def chunks_of(count):
    return range(0, count, CHUNK)


def is_early(base, count):
    return CHUNK <= base < min((1 + EARLY) * CHUNK, count - CHUNK)


def early_kernel(
    x_ref, table_ref, nbr_ref, code_ref, rcode_ref, route_ref, mix_ref, restrict_ref,
    y_ref, done_ref, acc_ref,
    nbr, code, rcode, route, mix, restrict, counts_ref, in_sems,
):
    count, channels, cells = x_ref.shape
    rotations = table_ref.shape[0]
    extended = count + 2 * RIM
    copies = fetched(
        (nbr_ref, code_ref, rcode_ref, route_ref, mix_ref, restrict_ref),
        (nbr, code, rcode, route, mix, restrict), in_sems,
    )
    acc_ref[...] = jnp.zeros(acc_ref.shape, F32)
    for base in chunks_of(count):
        rows = x_ref[base:base + CHUNK].reshape(CHUNK * channels, cells)
        for r in range(rotations):
            product = dot(rows, table_ref[r]).astype(BF16)
            y_ref[pl.ds(r * extended + RIM + base, CHUNK)] = product.reshape(CHUNK, channels, cells)
    for copy in copies:
        copy.wait()
    level = Level((nbr, code, rcode, route), y_ref, x_ref, mix, restrict, done_ref, acc_ref, counts_ref)
    for base in chunks_of(count):
        if is_early(base, count):
            level.run(base)
            level.pack(base)
        else:
            level.pass_over(base)


def late_kernel(
    x_ref, table_ref, nbr_ref, code_ref, rcode_ref, route_ref, mix_ref, restrict_ref,
    first_ref, second_ref, y_in_ref, done_in_ref, acc_in_ref, y_ref, done_ref, acc_ref, *refs,
):
    sent_refs, refs = refs[:-8], refs[-8:]
    nbr, code, rcode, route, mix, restrict, counts_ref, in_sems = refs
    del y_in_ref, done_in_ref, acc_in_ref
    count, channels, cells = x_ref.shape
    rotations = table_ref.shape[0]
    extended = count + 2 * RIM
    copies = fetched(
        (nbr_ref, code_ref, rcode_ref, route_ref, mix_ref, restrict_ref),
        (nbr, code, rcode, route, mix, restrict), in_sems,
    )
    right = faces_right()
    received = [first_ref[...], second_ref[...]]
    before = jnp.where(right, received[1], received[0])
    after = jnp.where(right, received[0], received[1])
    halo = jnp.concatenate([before, after], axis=0).reshape(2 * RIM * channels, cells)
    for r in range(rotations):
        product = dot(halo, table_ref[r]).astype(BF16).reshape(2 * RIM, channels, cells)
        y_ref[r * extended:r * extended + RIM] = product[:RIM]
        y_ref[r * extended + RIM + count:(r + 1) * extended] = product[RIM:]
    for copy in copies:
        copy.wait()
    level = Level((nbr, code, rcode, route), y_ref, x_ref, mix, restrict, done_ref, acc_ref, counts_ref)
    for base in chunks_of(count):
        if is_early(base, count):
            level.pass_over(base)
        else:
            level.run(base)
            level.pack(base)
    packing = Packing(count // level.tiles, level.cq, channels)
    half = LANES // 2
    lane = lax.broadcasted_iota(jnp.int32, (channels // 2, LANES), 1)
    for hop in range(level.tiles):
        out = sent_refs[hop]
        at = hop * packing.parts
        for p in range(packing.full):
            out[p * channels:(p + 1) * channels] = acc_ref[at + p].astype(BF16)
        if packing.half:
            value = acc_ref[at + packing.full]
            lower = pltpu.roll(value[channels // 2:], half, axis=1)
            joined = jnp.where(lane < half, value[:channels // 2], lower)
            out[packing.full * channels:] = joined.astype(BF16)


def order_kernel(cq, route_ref, done_ref, order_ref, skip_ref, sems):
    count, channels = done_ref.shape[:2]
    copies = [
        pltpu.make_async_copy(
            done_ref.at[pl.ds(base, CHUNK)], skip_ref.at[pl.ds(base, CHUNK)], sems.at[base // CHUNK]
        )
        for base in chunks_of(count)
    ]
    for copy in copies:
        copy.start()
    blocks = route_ref.shape[1]
    tiles = blocks // count
    packing = Packing(count // tiles, cq, channels)
    me = lax.axis_index("tile")
    base = me * count
    route = route_ref[...]
    mine = jnp.where((route >= base) & (route < base + count), 1.0, 0.0)
    shape = (blocks, blocks)
    of, at = (lax.broadcasted_iota(jnp.int32, shape, d) for d in (0, 1))
    earlier = jnp.where((of < at) & (lax.div(of, count) == lax.div(at, count)), 1.0, 0.0)
    rank = dot(jnp.broadcast_to(mine, (8, blocks)).astype(BF16), earlier.astype(BF16))[:1].astype(jnp.int32)
    source = lax.div(lax.broadcasted_iota(jnp.int32, (1, blocks), 1), count)
    hop = hop_between(me, source, tiles)
    column = packing.column(tiles, hop, rank).astype(F32)
    cells = count * cq
    cell = lax.broadcasted_iota(jnp.int32, (cells, blocks), 0)
    found = jnp.where(route == base + lax.div(cell, cq), column, 0.0)
    wanted = jnp.sum(found, axis=1, keepdims=True)
    wanted = wanted + lax.rem(lax.broadcasted_iota(jnp.int32, (cells, 1), 0), cq).astype(F32)
    across = jnp.transpose(jnp.broadcast_to(wanted, (cells, LANES)))[:1].astype(jnp.int32)
    step = LANES
    for row in range(0, order_ref.shape[0], step):
        index = row + lax.broadcasted_iota(jnp.int32, (step, cells), 0)
        order_ref[row:row + step] = jnp.where(index == across, 1.0, 0.0).astype(BF16)
    for copy in copies:
        copy.wait()


def merge_kernel(per, cq, order_ref, *refs):
    arrived, (coarse_ref, first_ref, second_ref) = refs[:-3], refs[-3:]
    order = hop_order(len(arrived))
    arrived = [arrived[0]] + [arrived[1 + order.index(hop)] for hop in range(1, len(arrived))]
    blocks, channels, cells = coarse_ref.shape
    tiles = len(arrived)
    packing = Packing(per, cq, channels)
    columns = [ref[p * channels:(p + 1) * channels] for ref in arrived for p in range(packing.full)]
    if packing.half:
        half = LANES // 2
        lane = lax.broadcasted_iota(jnp.int32, (channels // 2, LANES), 1)
        halves = [ref[packing.full * channels:].astype(F32) for ref in arrived]
        halves += [jnp.zeros_like(halves[0])] * (tiles % 2)
        for one, other in zip(halves[::2], halves[1::2]):
            upper = jnp.where(lane < half, one, pltpu.roll(other, half, axis=1))
            lower = jnp.where(lane < half, pltpu.roll(one, half, axis=1), other)
            columns.append(jnp.concatenate([upper, lower], axis=0).astype(BF16))
    joined = jnp.concatenate(columns, axis=1)
    values = [
        dot(joined, order_ref[:, c * cells:(c + 1) * cells]).astype(BF16) for c in range(blocks)
    ]
    for c in range(blocks):
        coarse_ref[c] = values[c]
    right = faces_right()
    first_ref[...] = jnp.where(right, values[-1], values[0])
    second_ref[...] = jnp.where(right, values[0], values[-1])


def inside_kernel(code_ref, coarse_ref, spatial_ref, mix_ref, total_ref, table_ref):
    blocks = coarse_ref.shape[0]
    values = [coarse_ref[c] for c in range(blocks)]
    for c in range(blocks):
        total = dot(mix_ref[0], values[c])
        for e, other in enumerate((c - 1, c + 1)):
            if 0 <= other < blocks:
                edge = dot(values[other], spatial_ref[code_ref[c, 0, e]]).astype(BF16)
                total = total + dot(mix_ref[e + 1], edge)
        total_ref[c] = total
        table_ref[2 + c] = spatial_ref[code_ref[c, 0, 2]]
    table_ref[0] = spatial_ref[code_ref[0, 0, 0]]
    table_ref[1] = spatial_ref[code_ref[blocks - 1, 0, 1]]


def coarse_kernel(seam_ref, second_ref, first_ref, coarse_ref, total_ref, table_ref, mix_ref, out_ref):
    blocks = coarse_ref.shape[0]
    right = faces_right()
    left_rows = jnp.where(right, second_ref[...], first_ref[...])
    right_rows = jnp.where(right, first_ref[...], second_ref[...])
    left_edge = dot(left_rows, table_ref[0]).astype(BF16)
    right_edge = dot(right_rows, table_ref[1]).astype(BF16)
    for c in range(blocks):
        total = total_ref[c] + dot(mix_ref[3], dot(seam_ref[c], table_ref[2 + c]).astype(BF16))
        if c == 0:
            total = total + dot(mix_ref[1], left_edge)
        if c == blocks - 1:
            total = total + dot(mix_ref[2], right_edge)
        out_ref[c] = (coarse_ref[c].astype(F32) + silu(total)).astype(BF16)


def params(mib=VMEM_MIB):
    return pltpu.CompilerParams(vmem_limit_bytes=mib * 1024 * 1024)


def per_device(
    fine, conv_spatial, conv_mix, neighbours, fine_codes, restrict, restrict_codes, route,
    coarse_spatial, coarse_mix, coarse_codes,
):
    x = fine[0, 0]
    count, channels, cells = x.shape
    rotations = conv_spatial.shape[0]
    cq = restrict.shape[2]
    tiles = route.shape[1] // count
    per = count // tiles
    blocks = count * cq // cells
    packing = Packing(per, cq, channels)
    nbr, codes = neighbours.transpose(2, 0, 1), fine_codes.transpose(2, 0, 1)
    narrow = restrict.transpose(0, 2, 1)

    rim_shape = jax.ShapeDtypeStruct((RIM, channels, cells), BF16)
    first, second = pl.pallas_call(
        cut_kernel,
        out_shape=(rim_shape, rim_shape),
        in_specs=[VMEM()] * 2,
        out_specs=(VMEM(),) * 2,
        compiler_params=params(),
        cost_estimate=pl.CostEstimate(flops=4 * 10**9, bytes_accessed=10**6, transcendentals=0),
        name="cut",
    )(x[:RIM], x[count - RIM:])
    second = swapped(False, second, "tile")
    first = swapped(True, first, "tile")

    y_shape = (rotations * (count + 2 * RIM), channels, cells)
    steps = count // CHUNK
    tables = (nbr, codes, restrict_codes, route)
    shared = [pltpu.SMEM(a.shape, jnp.int32) for a in tables] + [
        pltpu.VMEM(conv_mix.shape, BF16),
        pltpu.VMEM(narrow.shape, BF16),
        pltpu.SMEM((tiles,), jnp.int32),
        pltpu.SemaphoreType.DMA((6,)),
    ]
    made = (
        jax.ShapeDtypeStruct(y_shape, BF16),
        jax.ShapeDtypeStruct(x.shape, BF16),
        jax.ShapeDtypeStruct((tiles * packing.parts, channels, LANES), F32),
    )
    given = (x, conv_spatial) + tables + (conv_mix, narrow)
    given_specs = [VMEM()] * 2 + [ANY()] * 6
    y, done, acc = pl.pallas_call(
        early_kernel,
        out_shape=made,
        in_specs=given_specs,
        out_specs=(VMEM(), VMEM(), VMEM()),
        scratch_shapes=shared,
        compiler_params=params(),
        cost_estimate=pl.CostEstimate(flops=4 * 10**9, bytes_accessed=4 * 10**6, transcendentals=10**6),
        name="early",
    )(*given)

    sent_shape = jax.ShapeDtypeStruct((packing.rows, LANES), BF16)
    _, done, _, *sent = pl.pallas_call(
        late_kernel,
        out_shape=made + (sent_shape,) * tiles,
        in_specs=given_specs + [VMEM()] * 5,
        out_specs=(VMEM(),) * (3 + tiles),
        scratch_shapes=shared,
        input_output_aliases={10: 0, 11: 1, 12: 2},
        compiler_params=params(),
        name="late",
    )(*given, first, second, y, done, acc)

    order, skip = pl.pallas_call(
        functools.partial(order_kernel, cq),
        out_shape=(
            jax.ShapeDtypeStruct((packing.width(tiles), count * cq), BF16),
            jax.ShapeDtypeStruct(x.shape, BF16),
        ),
        in_specs=[VMEM(), VMEM()],
        out_specs=(VMEM(), ANY()),
        scratch_shapes=[pltpu.SemaphoreType.DMA((steps,))],
        compiler_params=params(),
        name="order",
    )(route, done)
    arrived = [sent[0]] + [exchanged(sent[hop], "tile", hop) for hop in range(1, tiles)]

    block_shape = jax.ShapeDtypeStruct((channels, cells), BF16)
    coarse, first, second = pl.pallas_call(
        functools.partial(merge_kernel, per, cq),
        out_shape=(jax.ShapeDtypeStruct((blocks, channels, cells), BF16), block_shape, block_shape),
        in_specs=[VMEM()] * (1 + tiles),
        out_specs=(VMEM(), VMEM(), VMEM()),
        compiler_params=params(),
        name="merge",
    )(order, arrived[0], *[arrived[hop] for hop in hop_order(tiles)])

    second = swapped(False, second, "tile")
    first = swapped(True, first, "tile")
    seam = shifted(coarse, "sect", 1)
    total, tables = pl.pallas_call(
        inside_kernel,
        out_shape=(
            jax.ShapeDtypeStruct(coarse.shape, F32),
            jax.ShapeDtypeStruct((2 + blocks,) + coarse_spatial.shape[1:], BF16),
        ),
        in_specs=[SMEM()] + [VMEM()] * 3,
        out_specs=(VMEM(), VMEM()),
        compiler_params=params(),
        name="inside",
    )(coarse_codes.transpose(1, 0, 2), coarse, coarse_spatial, coarse_mix)
    coarse_out = pl.pallas_call(
        coarse_kernel,
        out_shape=jax.ShapeDtypeStruct(coarse.shape, BF16),
        in_specs=[VMEM()] * 7,
        out_specs=VMEM(),
        compiler_params=params(),
        name="coarse",
    )(seam, second, first, coarse, total, tables, coarse_mix)
    return (skip[None, None], coarse_out[None, None])


def solution(mesh):
    data = P(("groups", "chan"), "sect", "tile", None, None)
    placed = (
        data,
        P(),
        P(),
        P("sect", "tile", None),
        P("sect", "tile", None),
        P(),
        P("sect", "tile"),
        P("sect", None),
        P(),
        P(),
        P("sect", "tile", None),
    )
    return jax.shard_map(
        per_device, mesh=mesh, in_specs=placed, out_specs=(data, data), check_vma=False
    )
```

```python
import functools

import jax
import jax.numpy as jnp
from jax import lax
from jax.experimental import pallas as pl
from jax.experimental.pallas import tpu as pltpu
from jax.sharding import PartitionSpec as P

LANES = 128
RIM = 2
CHUNK = 8
EARLY = 4
VMEM_MIB = 40

SMEM = functools.partial(pl.BlockSpec, memory_space=pltpu.SMEM)
VMEM = functools.partial(pl.BlockSpec, memory_space=pltpu.VMEM)
ANY = functools.partial(pl.BlockSpec, memory_space=pl.ANY)
HBM = functools.partial(pl.BlockSpec, memory_space=pltpu.HBM)
F32 = jnp.float32
BF16 = jnp.bfloat16


def dot(a, b):
    return jnp.dot(a, b, preferred_element_type=F32)


def silu(v):
    return v * (0.5 + 0.5 * jnp.tanh(0.5 * v))


def shifted(value, axis, steps):
    count = lax.axis_size(axis)
    return lax.ppermute(value, axis, [(i, (i + steps) % count) for i in range(count)])


def joined_mix(mix_ref, terms):
    return jnp.concatenate([mix_ref[t] for t in range(terms)], axis=1)


def dot_t(a, b):
    return lax.dot_general(a, b, (((1,), (1,)), ((), ())), preferred_element_type=F32)


def swapped(even, value, axis):
    count = lax.axis_size(axis)
    first = 0 if even else 1
    pairs = []
    for i in range(first, count + first, 2):
        here, there = i % count, (i + 1) % count
        pairs += [(here, there), (there, here)]
    return lax.ppermute(value, axis, pairs)


def paired(tiles):
    return tiles & (tiles - 1) == 0


def hop_between(dest, source, tiles):
    if paired(tiles):
        return lax.bitwise_xor(dest, source)
    return lax.rem(dest - source + tiles, tiles)


def exchanged(value, axis, hop):
    count = lax.axis_size(axis)
    pairs = [(i, i ^ hop if paired(count) else (i + hop) % count) for i in range(count)]
    return lax.ppermute(value, axis, pairs)


def hop_order(tiles):
    return list(range(tiles // 2, tiles)) + list(range(1, tiles // 2))


def faces_right():
    return lax.rem(lax.axis_index("tile"), 2) == 0


def mixed_skip(y_ref, y_index, taps, mix_wide, mix_ref, own):
    terms = [y_ref[y_index(t)] for t in range(taps)]
    wide = mix_wide.shape[1] // mix_ref.shape[1]
    mixed = dot(mix_wide, jnp.concatenate(terms[:wide], axis=0))
    for t in range(wide, taps):
        mixed = mixed + dot(mix_ref[t], terms[t])
    return (own.astype(F32) + silu(mixed)).astype(BF16)


def place(acc_ref, at, product, code, rank, cq):
    per = LANES // cq
    slot = lax.rem(rank, per)
    amount = lax.rem((slot - code) * cq + LANES, LANES)
    turned = pltpu.roll(product, amount, axis=1)
    lane = lax.broadcasted_iota(jnp.int32, turned.shape, 1)
    at = at + lax.div(rank, per)
    acc_ref[at] = jnp.where(lax.div(lane, cq) == slot, turned, acc_ref[at])


class Packing:
    def __init__(self, per, cq, channels):
        self.cq, self.channels = cq, channels
        self.lanes = LANES // cq
        self.full, left = divmod(per, self.lanes)
        self.half = 0 < left * 2 <= self.lanes
        if left and not self.half:
            self.full += 1
        self.parts = self.full + self.half
        self.rows = self.full * channels + (channels // 2 if self.half else 0)

    def width(self, tiles):
        return (tiles * self.full + (-(-tiles // 2) if self.half else 0)) * LANES

    def column(self, tiles, hop, rank):
        whole = (hop * self.full * self.lanes + rank) * self.cq
        if not self.half:
            return whole
        split = (
            (tiles * self.full + hop // 2) * LANES
            + hop % 2 * (LANES // 2)
            + (rank - self.full * self.lanes) * self.cq
        )
        return jnp.where(rank < self.full * self.lanes, whole, split)


def cut_kernel(head_ref, tail_ref, first_ref, second_ref):
    right = faces_right()
    head, tail = head_ref[...], tail_ref[...]
    first_ref[...] = jnp.where(right, tail, head)
    second_ref[...] = jnp.where(right, head, tail)


class Level:
    def __init__(self, tables, y_ref, x_ref, mix_ref, restrict_ref, done_ref, acc_ref, counts_ref):
        self.nbr, self.code, self.rcode, self.route = tables
        self.y, self.x, self.mix, self.done, self.acc, self.counts = y_ref, x_ref, mix_ref, done_ref, acc_ref, counts_ref
        self.count, self.channels, self.cells = x_ref.shape
        self.rotations, self.cq = restrict_ref.shape[:2]
        self.taps = mix_ref.shape[0]
        self.blocks = self.route.shape[1]
        self.tiles = self.blocks // self.count
        self.extended = self.count + 2 * RIM
        self.me = lax.axis_index("tile")
        self.mix_wide = joined_mix(mix_ref, min(self.taps, self.cells // self.channels))
        restricts = restrict_ref[...].reshape(self.rotations * self.cq, self.cells)
        self.stacked = jnp.concatenate([restricts] * (LANES // (self.rotations * self.cq)), axis=0)
        for d in range(self.tiles):
            counts_ref[d] = 0

    def y_index(self, b, t):
        local = self.nbr[t, 0, b] - self.me * self.count + RIM
        local = jnp.where(local < 0, local + self.blocks, local)
        local = jnp.where(local >= self.blocks, local - self.blocks, local)
        return self.code[t, 0, b] * self.extended + local

    def pass_over(self, base, store=None):
        for i in range(CHUNK):
            b = base + i
            dest = lax.div(self.route[0, self.me * self.count + b], self.count)
            rank = self.counts[dest]
            self.counts[dest] = rank + 1
            if store is not None:
                store(i, b, dest, rank)

    def run(self, base):
        for i in range(CHUNK):
            b = base + i
            self.done[b] = mixed_skip(
                self.y, functools.partial(self.y_index, b), self.taps, self.mix_wide, self.mix, self.x[b]
            )

    def pack(self, base):
        rows = self.done[base:base + CHUNK].reshape(CHUNK * self.channels, self.cells)
        products = dot_t(rows, self.stacked)
        parts = self.acc.shape[0] // self.tiles

        def store(i, b, dest, rank):
            hop = hop_between(dest, self.me, self.tiles)
            product = products[i * self.channels:(i + 1) * self.channels]
            place(self.acc, hop * parts, product, self.rcode[0, b], rank, self.cq)

        self.pass_over(base, store)


def fetched(sources, targets, sems):
    copies = [
        pltpu.make_async_copy(source, target, sems.at[i])
        for i, (source, target) in enumerate(zip(sources, targets))
    ]
    for copy in copies:
        copy.start()
    return copies


def chunks_of(count):
    return range(0, count, CHUNK)


def is_early(base, count):
    return CHUNK <= base < min((1 + EARLY) * CHUNK, count - CHUNK)


def early_kernel(
    x_ref, table_ref, nbr_ref, code_ref, rcode_ref, route_ref, mix_ref, restrict_ref,
    y_ref, done_ref, acc_ref,
    nbr, code, rcode, route, mix, restrict, counts_ref, in_sems,
):
    count, channels, cells = x_ref.shape
    rotations = table_ref.shape[0]
    extended = count + 2 * RIM
    copies = fetched(
        (nbr_ref, code_ref, rcode_ref, route_ref, mix_ref, restrict_ref),
        (nbr, code, rcode, route, mix, restrict), in_sems,
    )
    acc_ref[...] = jnp.zeros(acc_ref.shape, F32)
    rows = x_ref[...].reshape(count * channels, cells)
    for r in range(rotations):
        product = dot(rows, table_ref[r]).astype(BF16)
        y_ref[pl.ds(r * extended + RIM, count)] = product.reshape(count, channels, cells)
    for copy in copies:
        copy.wait()
    level = Level((nbr, code, rcode, route), y_ref, x_ref, mix, restrict, done_ref, acc_ref, counts_ref)
    for base in chunks_of(count):
        if is_early(base, count):
            level.run(base)
            level.pack(base)
        else:
            level.pass_over(base)


def late_kernel(
    x_ref, table_ref, nbr_ref, code_ref, rcode_ref, route_ref, mix_ref, restrict_ref,
    first_ref, second_ref, y_in_ref, done_in_ref, acc_in_ref, y_ref, done_ref, acc_ref, *refs,
):
    sent_refs, refs = refs[:-8], refs[-8:]
    nbr, code, rcode, route, mix, restrict, counts_ref, in_sems = refs
    del y_in_ref, done_in_ref, acc_in_ref
    count, channels, cells = x_ref.shape
    rotations = table_ref.shape[0]
    extended = count + 2 * RIM
    copies = fetched(
        (nbr_ref, code_ref, rcode_ref, route_ref, mix_ref, restrict_ref),
        (nbr, code, rcode, route, mix, restrict), in_sems,
    )
    right = faces_right()
    received = [first_ref[...], second_ref[...]]
    before = jnp.where(right, received[1], received[0])
    after = jnp.where(right, received[0], received[1])
    halo = jnp.concatenate([before, after], axis=0).reshape(2 * RIM * channels, cells)
    for r in range(rotations):
        product = dot(halo, table_ref[r]).astype(BF16).reshape(2 * RIM, channels, cells)
        y_ref[r * extended:r * extended + RIM] = product[:RIM]
        y_ref[r * extended + RIM + count:(r + 1) * extended] = product[RIM:]
    for copy in copies:
        copy.wait()
    level = Level((nbr, code, rcode, route), y_ref, x_ref, mix, restrict, done_ref, acc_ref, counts_ref)
    for base in chunks_of(count):
        if is_early(base, count):
            level.pass_over(base)
        else:
            level.run(base)
            level.pack(base)
    packing = Packing(count // level.tiles, level.cq, channels)
    half = LANES // 2
    lane = lax.broadcasted_iota(jnp.int32, (channels // 2, LANES), 1)
    for hop in range(level.tiles):
        out = sent_refs[hop]
        at = hop * packing.parts
        for p in range(packing.full):
            out[p * channels:(p + 1) * channels] = acc_ref[at + p].astype(BF16)
        if packing.half:
            value = acc_ref[at + packing.full]
            lower = pltpu.roll(value[channels // 2:], half, axis=1)
            joined = jnp.where(lane < half, value[:channels // 2], lower)
            out[packing.full * channels:] = joined.astype(BF16)


def order_kernel(cq, route_ref, done_ref, order_ref, skip_ref, sems):
    count, channels = done_ref.shape[:2]
    copies = [
        pltpu.make_async_copy(
            done_ref.at[pl.ds(base, CHUNK)], skip_ref.at[pl.ds(base, CHUNK)], sems.at[base // CHUNK]
        )
        for base in chunks_of(count)
    ]
    for copy in copies:
        copy.start()
    blocks = route_ref.shape[1]
    tiles = blocks // count
    packing = Packing(count // tiles, cq, channels)
    me = lax.axis_index("tile")
    base = me * count
    route = route_ref[...]
    mine = jnp.where((route >= base) & (route < base + count), 1.0, 0.0)
    shape = (blocks, blocks)
    of, at = (lax.broadcasted_iota(jnp.int32, shape, d) for d in (0, 1))
    earlier = jnp.where((of < at) & (lax.div(of, count) == lax.div(at, count)), 1.0, 0.0)
    rank = dot(jnp.broadcast_to(mine, (8, blocks)).astype(BF16), earlier.astype(BF16))[:1].astype(jnp.int32)
    source = lax.div(lax.broadcasted_iota(jnp.int32, (1, blocks), 1), count)
    hop = hop_between(me, source, tiles)
    column = packing.column(tiles, hop, rank).astype(F32)
    cells = count * cq
    cell = lax.broadcasted_iota(jnp.int32, (cells, blocks), 0)
    found = jnp.where(route == base + lax.div(cell, cq), column, 0.0)
    wanted = jnp.sum(found, axis=1, keepdims=True)
    wanted = wanted + lax.rem(lax.broadcasted_iota(jnp.int32, (cells, 1), 0), cq).astype(F32)
    across = jnp.transpose(jnp.broadcast_to(wanted, (cells, LANES)))[:1].astype(jnp.int32)
    step = LANES
    for row in range(0, order_ref.shape[0], step):
        index = row + lax.broadcasted_iota(jnp.int32, (step, cells), 0)
        order_ref[row:row + step] = jnp.where(index == across, 1.0, 0.0).astype(BF16)
    for copy in copies:
        copy.wait()


def merge_kernel(per, cq, order_ref, *refs):
    arrived, (coarse_ref, first_ref, second_ref) = refs[:-3], refs[-3:]
    order = hop_order(len(arrived))
    arrived = [arrived[0]] + [arrived[1 + order.index(hop)] for hop in range(1, len(arrived))]
    blocks, channels, cells = coarse_ref.shape
    tiles = len(arrived)
    packing = Packing(per, cq, channels)
    columns = [ref[p * channels:(p + 1) * channels] for ref in arrived for p in range(packing.full)]
    if packing.half:
        half = LANES // 2
        lane = lax.broadcasted_iota(jnp.int32, (channels // 2, LANES), 1)
        halves = [ref[packing.full * channels:].astype(F32) for ref in arrived]
        halves += [jnp.zeros_like(halves[0])] * (tiles % 2)
        for one, other in zip(halves[::2], halves[1::2]):
            upper = jnp.where(lane < half, one, pltpu.roll(other, half, axis=1))
            lower = jnp.where(lane < half, pltpu.roll(one, half, axis=1), other)
            columns.append(jnp.concatenate([upper, lower], axis=0).astype(BF16))
    joined = jnp.concatenate(columns, axis=1)
    values = [
        dot(joined, order_ref[:, c * cells:(c + 1) * cells]).astype(BF16) for c in range(blocks)
    ]
    for c in range(blocks):
        coarse_ref[c] = values[c]
    right = faces_right()
    first_ref[...] = jnp.where(right, values[-1], values[0])
    second_ref[...] = jnp.where(right, values[0], values[-1])


def inside_kernel(code_ref, coarse_ref, spatial_ref, mix_ref, total_ref, table_ref):
    blocks = coarse_ref.shape[0]
    values = [coarse_ref[c] for c in range(blocks)]
    for c in range(blocks):
        total = dot(mix_ref[0], values[c])
        for e, other in enumerate((c - 1, c + 1)):
            if 0 <= other < blocks:
                edge = dot(values[other], spatial_ref[code_ref[c, 0, e]]).astype(BF16)
                total = total + dot(mix_ref[e + 1], edge)
        total_ref[c] = total
        table_ref[2 + c] = spatial_ref[code_ref[c, 0, 2]]
    table_ref[0] = spatial_ref[code_ref[0, 0, 0]]
    table_ref[1] = spatial_ref[code_ref[blocks - 1, 0, 1]]


def coarse_kernel(seam_ref, second_ref, first_ref, coarse_ref, total_ref, table_ref, mix_ref, out_ref):
    blocks = coarse_ref.shape[0]
    right = faces_right()
    left_rows = jnp.where(right, second_ref[...], first_ref[...])
    right_rows = jnp.where(right, first_ref[...], second_ref[...])
    left_edge = dot(left_rows, table_ref[0]).astype(BF16)
    right_edge = dot(right_rows, table_ref[1]).astype(BF16)
    for c in range(blocks):
        total = total_ref[c] + dot(mix_ref[3], dot(seam_ref[c], table_ref[2 + c]).astype(BF16))
        if c == 0:
            total = total + dot(mix_ref[1], left_edge)
        if c == blocks - 1:
            total = total + dot(mix_ref[2], right_edge)
        out_ref[c] = (coarse_ref[c].astype(F32) + silu(total)).astype(BF16)


def params(mib=VMEM_MIB):
    return pltpu.CompilerParams(vmem_limit_bytes=mib * 1024 * 1024)


def per_device(
    fine, conv_spatial, conv_mix, neighbours, fine_codes, restrict, restrict_codes, route,
    coarse_spatial, coarse_mix, coarse_codes,
):
    x = fine[0, 0]
    count, channels, cells = x.shape
    rotations = conv_spatial.shape[0]
    cq = restrict.shape[2]
    tiles = route.shape[1] // count
    per = count // tiles
    blocks = count * cq // cells
    packing = Packing(per, cq, channels)
    nbr, codes = neighbours.transpose(2, 0, 1), fine_codes.transpose(2, 0, 1)
    narrow = restrict.transpose(0, 2, 1)

    rim_shape = jax.ShapeDtypeStruct((RIM, channels, cells), BF16)
    first, second = pl.pallas_call(
        cut_kernel,
        out_shape=(rim_shape, rim_shape),
        in_specs=[VMEM()] * 2,
        out_specs=(VMEM(),) * 2,
        compiler_params=params(),
        cost_estimate=pl.CostEstimate(flops=4 * 10**9, bytes_accessed=10**6, transcendentals=0),
        name="cut",
    )(x[:RIM], x[count - RIM:])
    second = swapped(False, second, "tile")
    first = swapped(True, first, "tile")

    y_shape = (rotations * (count + 2 * RIM), channels, cells)
    steps = count // CHUNK
    tables = (nbr, codes, restrict_codes, route)
    shared = [pltpu.SMEM(a.shape, jnp.int32) for a in tables] + [
        pltpu.VMEM(conv_mix.shape, BF16),
        pltpu.VMEM(narrow.shape, BF16),
        pltpu.SMEM((tiles,), jnp.int32),
        pltpu.SemaphoreType.DMA((6,)),
    ]
    made = (
        jax.ShapeDtypeStruct(y_shape, BF16),
        jax.ShapeDtypeStruct(x.shape, BF16),
        jax.ShapeDtypeStruct((tiles * packing.parts, channels, LANES), F32),
    )
    given = (x, conv_spatial) + tables + (conv_mix, narrow)
    given_specs = [VMEM()] * 2 + [ANY()] * 6
    y, done, acc = pl.pallas_call(
        early_kernel,
        out_shape=made,
        in_specs=given_specs,
        out_specs=(VMEM(), VMEM(), VMEM()),
        scratch_shapes=shared,
        compiler_params=params(),
        cost_estimate=pl.CostEstimate(flops=4 * 10**9, bytes_accessed=4 * 10**6, transcendentals=10**6),
        name="early",
    )(*given)

    sent_shape = jax.ShapeDtypeStruct((packing.rows, LANES), BF16)
    _, done, _, *sent = pl.pallas_call(
        late_kernel,
        out_shape=made + (sent_shape,) * tiles,
        in_specs=given_specs + [VMEM()] * 5,
        out_specs=(VMEM(),) * (3 + tiles),
        scratch_shapes=shared,
        input_output_aliases={10: 0, 11: 1, 12: 2},
        compiler_params=params(),
        name="late",
    )(*given, first, second, y, done, acc)

    order, skip = pl.pallas_call(
        functools.partial(order_kernel, cq),
        out_shape=(
            jax.ShapeDtypeStruct((packing.width(tiles), count * cq), BF16),
            jax.ShapeDtypeStruct(x.shape, BF16),
        ),
        in_specs=[VMEM(), VMEM()],
        out_specs=(VMEM(), ANY()),
        scratch_shapes=[pltpu.SemaphoreType.DMA((steps,))],
        compiler_params=params(),
        name="order",
    )(route, done)
    arrived = [sent[0]] + [exchanged(sent[hop], "tile", hop) for hop in range(1, tiles)]

    block_shape = jax.ShapeDtypeStruct((channels, cells), BF16)
    coarse, first, second = pl.pallas_call(
        functools.partial(merge_kernel, per, cq),
        out_shape=(jax.ShapeDtypeStruct((blocks, channels, cells), BF16), block_shape, block_shape),
        in_specs=[VMEM()] * (1 + tiles),
        out_specs=(VMEM(), VMEM(), VMEM()),
        compiler_params=params(),
        name="merge",
    )(order, arrived[0], *[arrived[hop] for hop in hop_order(tiles)])

    second = swapped(False, second, "tile")
    first = swapped(True, first, "tile")
    seam = shifted(coarse, "sect", 1)
    total, tables = pl.pallas_call(
        inside_kernel,
        out_shape=(
            jax.ShapeDtypeStruct(coarse.shape, F32),
            jax.ShapeDtypeStruct((2 + blocks,) + coarse_spatial.shape[1:], BF16),
        ),
        in_specs=[SMEM()] + [VMEM()] * 3,
        out_specs=(VMEM(), VMEM()),
        compiler_params=params(),
        name="inside",
    )(coarse_codes.transpose(1, 0, 2), coarse, coarse_spatial, coarse_mix)
    coarse_out = pl.pallas_call(
        coarse_kernel,
        out_shape=jax.ShapeDtypeStruct(coarse.shape, BF16),
        in_specs=[VMEM()] * 7,
        out_specs=VMEM(),
        compiler_params=params(),
        name="coarse",
    )(seam, second, first, coarse, total, tables, coarse_mix)
    return (skip[None, None], coarse_out[None, None])


def solution(mesh):
    data = P(("groups", "chan"), "sect", "tile", None, None)
    placed = (
        data,
        P(),
        P(),
        P("sect", "tile", None),
        P("sect", "tile", None),
        P(),
        P("sect", "tile"),
        P("sect", None),
        P(),
        P(),
        P("sect", "tile", None),
    )
    return jax.shard_map(
        per_device, mesh=mesh, in_specs=placed, out_specs=(data, data), check_vma=False
    )
```

```python
import functools

import jax
import jax.numpy as jnp
from jax import lax
from jax.experimental import pallas as pl
from jax.experimental.pallas import tpu as pltpu
from jax.sharding import PartitionSpec as P

LANES = 128
RIM = 2
CHUNK = 8
EARLY = 4
VMEM_MIB = 40

SMEM = functools.partial(pl.BlockSpec, memory_space=pltpu.SMEM)
VMEM = functools.partial(pl.BlockSpec, memory_space=pltpu.VMEM)
ANY = functools.partial(pl.BlockSpec, memory_space=pl.ANY)
HBM = functools.partial(pl.BlockSpec, memory_space=pltpu.HBM)
F32 = jnp.float32
BF16 = jnp.bfloat16


def dot(a, b):
    return jnp.dot(a, b, preferred_element_type=F32)


def silu(v):
    return v * (0.5 + 0.5 * jnp.tanh(0.5 * v))


def shifted(value, axis, steps):
    count = lax.axis_size(axis)
    return lax.ppermute(value, axis, [(i, (i + steps) % count) for i in range(count)])


def joined_mix(mix_ref, terms):
    return jnp.concatenate([mix_ref[t] for t in range(terms)], axis=1)


def dot_t(a, b):
    return lax.dot_general(a, b, (((1,), (1,)), ((), ())), preferred_element_type=F32)


def swapped(even, value, axis):
    count = lax.axis_size(axis)
    first = 0 if even else 1
    pairs = []
    for i in range(first, count + first, 2):
        here, there = i % count, (i + 1) % count
        pairs += [(here, there), (there, here)]
    return lax.ppermute(value, axis, pairs)


def paired(tiles):
    return tiles & (tiles - 1) == 0


def hop_between(dest, source, tiles):
    if paired(tiles):
        return lax.bitwise_xor(dest, source)
    return lax.rem(dest - source + tiles, tiles)


def exchanged(value, axis, hop):
    count = lax.axis_size(axis)
    pairs = [(i, i ^ hop if paired(count) else (i + hop) % count) for i in range(count)]
    return lax.ppermute(value, axis, pairs)


def hop_order(tiles):
    return list(range(tiles // 2, tiles)) + list(range(1, tiles // 2))


def faces_right():
    return lax.rem(lax.axis_index("tile"), 2) == 0


def mixed_skip(y_ref, y_index, taps, mix_wide, mix_ref, own):
    terms = [y_ref[y_index(t)] for t in range(taps)]
    wide = mix_wide.shape[1] // mix_ref.shape[1]
    mixed = dot(mix_wide, jnp.concatenate(terms[:wide], axis=0))
    for t in range(wide, taps):
        mixed = mixed + dot(mix_ref[t], terms[t])
    return (own.astype(F32) + silu(mixed)).astype(BF16)


def place(acc_ref, at, product, code, rank, cq):
    per = LANES // cq
    slot = lax.rem(rank, per)
    amount = lax.rem((slot - code) * cq + LANES, LANES)
    turned = pltpu.roll(product, amount, axis=1)
    lane = lax.broadcasted_iota(jnp.int32, turned.shape, 1)
    at = at + lax.div(rank, per)
    acc_ref[at] = jnp.where(lax.div(lane, cq) == slot, turned, acc_ref[at])


class Packing:
    def __init__(self, per, cq, channels):
        self.cq, self.channels = cq, channels
        self.lanes = LANES // cq
        self.full, left = divmod(per, self.lanes)
        self.half = 0 < left * 2 <= self.lanes
        if left and not self.half:
            self.full += 1
        self.parts = self.full + self.half
        self.rows = self.full * channels + (channels // 2 if self.half else 0)

    def width(self, tiles):
        return (tiles * self.full + (-(-tiles // 2) if self.half else 0)) * LANES

    def column(self, tiles, hop, rank):
        whole = (hop * self.full * self.lanes + rank) * self.cq
        if not self.half:
            return whole
        split = (
            (tiles * self.full + hop // 2) * LANES
            + hop % 2 * (LANES // 2)
            + (rank - self.full * self.lanes) * self.cq
        )
        return jnp.where(rank < self.full * self.lanes, whole, split)


def cut_kernel(head_ref, tail_ref, first_ref, second_ref):
    right = faces_right()
    head, tail = head_ref[...], tail_ref[...]
    first_ref[...] = jnp.where(right, tail, head)
    second_ref[...] = jnp.where(right, head, tail)


class Level:
    def __init__(self, tables, y_ref, x_ref, mix_ref, restrict_ref, done_ref, acc_ref, counts_ref):
        self.nbr, self.code, self.rcode, self.route = tables
        self.y, self.x, self.mix, self.done, self.acc, self.counts = y_ref, x_ref, mix_ref, done_ref, acc_ref, counts_ref
        self.count, self.channels, self.cells = x_ref.shape
        self.rotations, self.cq = restrict_ref.shape[:2]
        self.taps = mix_ref.shape[0]
        self.blocks = self.route.shape[1]
        self.tiles = self.blocks // self.count
        self.extended = self.count + 2 * RIM
        self.me = lax.axis_index("tile")
        self.mix_wide = joined_mix(mix_ref, min(self.taps, self.cells // self.channels))
        restricts = restrict_ref[...].reshape(self.rotations * self.cq, self.cells)
        self.stacked = jnp.concatenate([restricts] * (LANES // (self.rotations * self.cq)), axis=0)
        for d in range(self.tiles):
            counts_ref[d] = 0

    def y_index(self, b, t):
        local = self.nbr[t, 0, b] - self.me * self.count + RIM
        local = jnp.where(local < 0, local + self.blocks, local)
        local = jnp.where(local >= self.blocks, local - self.blocks, local)
        return self.code[t, 0, b] * self.extended + local

    def pass_over(self, base, store=None):
        for i in range(CHUNK):
            b = base + i
            dest = lax.div(self.route[0, self.me * self.count + b], self.count)
            rank = self.counts[dest]
            self.counts[dest] = rank + 1
            if store is not None:
                store(i, b, dest, rank)

    def run(self, base):
        for i in range(CHUNK):
            b = base + i
            self.done[b] = mixed_skip(
                self.y, functools.partial(self.y_index, b), self.taps, self.mix_wide, self.mix, self.x[b]
            )

    def pack(self, base):
        rows = self.done[base:base + CHUNK].reshape(CHUNK * self.channels, self.cells)
        products = dot_t(rows, self.stacked)
        parts = self.acc.shape[0] // self.tiles

        def store(i, b, dest, rank):
            hop = hop_between(dest, self.me, self.tiles)
            product = products[i * self.channels:(i + 1) * self.channels]
            place(self.acc, hop * parts, product, self.rcode[0, b], rank, self.cq)

        self.pass_over(base, store)


def fetched(sources, targets, sems):
    copies = [
        pltpu.make_async_copy(source, target, sems.at[i])
        for i, (source, target) in enumerate(zip(sources, targets))
    ]
    for copy in copies:
        copy.start()
    return copies


def chunks_of(count):
    return range(0, count, CHUNK)


def is_early(base, count):
    return CHUNK <= base < min((1 + EARLY) * CHUNK, count - CHUNK)


def early_kernel(
    x_ref, table_ref, nbr_ref, code_ref, rcode_ref, route_ref, mix_ref, restrict_ref,
    y_ref, done_ref, acc_ref,
    nbr, code, rcode, route, mix, restrict, counts_ref, in_sems,
):
    count, channels, cells = x_ref.shape
    rotations = table_ref.shape[0]
    extended = count + 2 * RIM
    copies = fetched(
        (nbr_ref, code_ref, rcode_ref, route_ref, mix_ref, restrict_ref),
        (nbr, code, rcode, route, mix, restrict), in_sems,
    )
    acc_ref[...] = jnp.zeros(acc_ref.shape, F32)
    rows = x_ref[...].reshape(count * channels, cells)
    for r in range(rotations):
        product = dot(rows, table_ref[r]).astype(BF16)
        y_ref[pl.ds(r * extended + RIM, count)] = product.reshape(count, channels, cells)
    for copy in copies:
        copy.wait()
    level = Level((nbr, code, rcode, route), y_ref, x_ref, mix, restrict, done_ref, acc_ref, counts_ref)
    for base in chunks_of(count):
        if is_early(base, count):
            level.run(base)
            level.pack(base)
        else:
            level.pass_over(base)


def late_kernel(
    x_ref, table_ref, nbr_ref, code_ref, rcode_ref, route_ref, mix_ref, restrict_ref,
    first_ref, second_ref, y_in_ref, done_in_ref, acc_in_ref, y_ref, done_ref, acc_ref, *refs,
):
    sent_refs, refs = refs[:-8], refs[-8:]
    nbr, code, rcode, route, mix, restrict, counts_ref, in_sems = refs
    del y_in_ref, done_in_ref, acc_in_ref
    count, channels, cells = x_ref.shape
    rotations = table_ref.shape[0]
    extended = count + 2 * RIM
    copies = fetched(
        (nbr_ref, code_ref, rcode_ref, route_ref, mix_ref, restrict_ref),
        (nbr, code, rcode, route, mix, restrict), in_sems,
    )
    right = faces_right()
    received = [first_ref[...], second_ref[...]]
    before = jnp.where(right, received[1], received[0])
    after = jnp.where(right, received[0], received[1])
    halo = jnp.concatenate([before, after], axis=0).reshape(2 * RIM * channels, cells)
    for r in range(rotations):
        product = dot(halo, table_ref[r]).astype(BF16).reshape(2 * RIM, channels, cells)
        y_ref[r * extended:r * extended + RIM] = product[:RIM]
        y_ref[r * extended + RIM + count:(r + 1) * extended] = product[RIM:]
    for copy in copies:
        copy.wait()
    level = Level((nbr, code, rcode, route), y_ref, x_ref, mix, restrict, done_ref, acc_ref, counts_ref)
    for base in chunks_of(count):
        if is_early(base, count):
            level.pass_over(base)
        else:
            level.run(base)
            level.pack(base)
    packing = Packing(count // level.tiles, level.cq, channels)
    half = LANES // 2
    lane = lax.broadcasted_iota(jnp.int32, (channels // 2, LANES), 1)
    for hop in range(level.tiles):
        out = sent_refs[hop]
        at = hop * packing.parts
        for p in range(packing.full):
            out[p * channels:(p + 1) * channels] = acc_ref[at + p].astype(BF16)
        if packing.half:
            value = acc_ref[at + packing.full]
            lower = pltpu.roll(value[channels // 2:], half, axis=1)
            joined = jnp.where(lane < half, value[:channels // 2], lower)
            out[packing.full * channels:] = joined.astype(BF16)


def order_kernel(cq, route_ref, done_ref, order_ref, skip_ref, sems):
    count, channels = done_ref.shape[:2]
    copies = [
        pltpu.make_async_copy(
            done_ref.at[pl.ds(base, CHUNK)], skip_ref.at[pl.ds(base, CHUNK)], sems.at[base // CHUNK]
        )
        for base in chunks_of(count)
    ]
    for copy in copies:
        copy.start()
    blocks = route_ref.shape[1]
    tiles = blocks // count
    packing = Packing(count // tiles, cq, channels)
    me = lax.axis_index("tile")
    base = me * count
    route = route_ref[...]
    mine = jnp.where((route >= base) & (route < base + count), 1.0, 0.0)
    shape = (blocks, blocks)
    of, at = (lax.broadcasted_iota(jnp.int32, shape, d) for d in (0, 1))
    earlier = jnp.where((of < at) & (lax.div(of, count) == lax.div(at, count)), 1.0, 0.0)
    rank = dot(jnp.broadcast_to(mine, (8, blocks)).astype(BF16), earlier.astype(BF16))[:1].astype(jnp.int32)
    source = lax.div(lax.broadcasted_iota(jnp.int32, (1, blocks), 1), count)
    hop = hop_between(me, source, tiles)
    column = packing.column(tiles, hop, rank).astype(F32)
    cells = count * cq
    cell = lax.broadcasted_iota(jnp.int32, (cells, blocks), 0)
    found = jnp.where(route == base + lax.div(cell, cq), column, 0.0)
    wanted = jnp.sum(found, axis=1, keepdims=True)
    wanted = wanted + lax.rem(lax.broadcasted_iota(jnp.int32, (cells, 1), 0), cq).astype(F32)
    across = jnp.transpose(jnp.broadcast_to(wanted, (cells, LANES)))[:1].astype(jnp.int32)
    step = LANES
    for row in range(0, order_ref.shape[0], step):
        index = row + lax.broadcasted_iota(jnp.int32, (step, cells), 0)
        order_ref[row:row + step] = jnp.where(index == across, 1.0, 0.0).astype(BF16)
    for copy in copies:
        copy.wait()


def merge_kernel(per, cq, order_ref, *refs):
    arrived, (coarse_ref, first_ref, second_ref) = refs[:-3], refs[-3:]
    order = hop_order(len(arrived))
    arrived = [arrived[0]] + [arrived[1 + order.index(hop)] for hop in range(1, len(arrived))]
    blocks, channels, cells = coarse_ref.shape
    tiles = len(arrived)
    packing = Packing(per, cq, channels)
    columns = [ref[p * channels:(p + 1) * channels] for ref in arrived for p in range(packing.full)]
    if packing.half:
        half = LANES // 2
        lane = lax.broadcasted_iota(jnp.int32, (channels // 2, LANES), 1)
        halves = [ref[packing.full * channels:].astype(F32) for ref in arrived]
        halves += [jnp.zeros_like(halves[0])] * (tiles % 2)
        for one, other in zip(halves[::2], halves[1::2]):
            upper = jnp.where(lane < half, one, pltpu.roll(other, half, axis=1))
            lower = jnp.where(lane < half, pltpu.roll(one, half, axis=1), other)
            columns.append(jnp.concatenate([upper, lower], axis=0).astype(BF16))
    joined = jnp.concatenate(columns, axis=1)
    values = [
        dot(joined, order_ref[:, c * cells:(c + 1) * cells]).astype(BF16) for c in range(blocks)
    ]
    for c in range(blocks):
        coarse_ref[c] = values[c]
    right = faces_right()
    first_ref[...] = jnp.where(right, values[-1], values[0])
    second_ref[...] = jnp.where(right, values[0], values[-1])


def inside_kernel(code_ref, coarse_ref, spatial_ref, mix_ref, total_ref, table_ref):
    blocks = coarse_ref.shape[0]
    values = [coarse_ref[c] for c in range(blocks)]
    for c in range(blocks):
        total = dot(mix_ref[0], values[c])
        for e, other in enumerate((c - 1, c + 1)):
            if 0 <= other < blocks:
                edge = dot(values[other], spatial_ref[code_ref[c, 0, e]]).astype(BF16)
                total = total + dot(mix_ref[e + 1], edge)
        total_ref[c] = total
        table_ref[2 + c] = spatial_ref[code_ref[c, 0, 2]]
    table_ref[0] = spatial_ref[code_ref[0, 0, 0]]
    table_ref[1] = spatial_ref[code_ref[blocks - 1, 0, 1]]


def coarse_kernel(second_ref, seam_ref, first_ref, coarse_ref, total_ref, table_ref, mix_ref, out_ref):
    blocks = coarse_ref.shape[0]
    right = faces_right()
    left_rows = jnp.where(right, second_ref[...], first_ref[...])
    right_rows = jnp.where(right, first_ref[...], second_ref[...])
    left_edge = dot(left_rows, table_ref[0]).astype(BF16)
    right_edge = dot(right_rows, table_ref[1]).astype(BF16)
    for c in range(blocks):
        total = total_ref[c] + dot(mix_ref[3], dot(seam_ref[c], table_ref[2 + c]).astype(BF16))
        if c == 0:
            total = total + dot(mix_ref[1], left_edge)
        if c == blocks - 1:
            total = total + dot(mix_ref[2], right_edge)
        out_ref[c] = (coarse_ref[c].astype(F32) + silu(total)).astype(BF16)


def params(mib=VMEM_MIB):
    return pltpu.CompilerParams(vmem_limit_bytes=mib * 1024 * 1024)


def per_device(
    fine, conv_spatial, conv_mix, neighbours, fine_codes, restrict, restrict_codes, route,
    coarse_spatial, coarse_mix, coarse_codes,
):
    x = fine[0, 0]
    count, channels, cells = x.shape
    rotations = conv_spatial.shape[0]
    cq = restrict.shape[2]
    tiles = route.shape[1] // count
    per = count // tiles
    blocks = count * cq // cells
    packing = Packing(per, cq, channels)
    nbr, codes = neighbours.transpose(2, 0, 1), fine_codes.transpose(2, 0, 1)
    narrow = restrict.transpose(0, 2, 1)

    rim_shape = jax.ShapeDtypeStruct((RIM, channels, cells), BF16)
    first, second = pl.pallas_call(
        cut_kernel,
        out_shape=(rim_shape, rim_shape),
        in_specs=[VMEM()] * 2,
        out_specs=(VMEM(),) * 2,
        compiler_params=params(),
        cost_estimate=pl.CostEstimate(flops=4 * 10**9, bytes_accessed=10**6, transcendentals=0),
        name="cut",
    )(x[:RIM], x[count - RIM:])
    second = swapped(False, second, "tile")
    first = swapped(True, first, "tile")

    y_shape = (rotations * (count + 2 * RIM), channels, cells)
    steps = count // CHUNK
    tables = (nbr, codes, restrict_codes, route)
    shared = [pltpu.SMEM(a.shape, jnp.int32) for a in tables] + [
        pltpu.VMEM(conv_mix.shape, BF16),
        pltpu.VMEM(narrow.shape, BF16),
        pltpu.SMEM((tiles,), jnp.int32),
        pltpu.SemaphoreType.DMA((6,)),
    ]
    made = (
        jax.ShapeDtypeStruct(y_shape, BF16),
        jax.ShapeDtypeStruct(x.shape, BF16),
        jax.ShapeDtypeStruct((tiles * packing.parts, channels, LANES), F32),
    )
    given = (x, conv_spatial) + tables + (conv_mix, narrow)
    given_specs = [VMEM()] * 2 + [ANY()] * 6
    y, done, acc = pl.pallas_call(
        early_kernel,
        out_shape=made,
        in_specs=given_specs,
        out_specs=(VMEM(), VMEM(), VMEM()),
        scratch_shapes=shared,
        compiler_params=params(),
        cost_estimate=pl.CostEstimate(flops=4 * 10**9, bytes_accessed=4 * 10**6, transcendentals=10**6),
        name="early",
    )(*given)

    sent_shape = jax.ShapeDtypeStruct((packing.rows, LANES), BF16)
    _, done, _, *sent = pl.pallas_call(
        late_kernel,
        out_shape=made + (sent_shape,) * tiles,
        in_specs=given_specs + [VMEM()] * 5,
        out_specs=(VMEM(),) * (3 + tiles),
        scratch_shapes=shared,
        input_output_aliases={10: 0, 11: 1, 12: 2},
        compiler_params=params(),
        name="late",
    )(*given, first, second, y, done, acc)

    order, skip = pl.pallas_call(
        functools.partial(order_kernel, cq),
        out_shape=(
            jax.ShapeDtypeStruct((packing.width(tiles), count * cq), BF16),
            jax.ShapeDtypeStruct(x.shape, BF16),
        ),
        in_specs=[VMEM(), VMEM()],
        out_specs=(VMEM(), ANY()),
        scratch_shapes=[pltpu.SemaphoreType.DMA((steps,))],
        compiler_params=params(),
        name="order",
    )(route, done)
    arrived = [sent[0]] + [exchanged(sent[hop], "tile", hop) for hop in range(1, tiles)]

    block_shape = jax.ShapeDtypeStruct((channels, cells), BF16)
    coarse, first, second = pl.pallas_call(
        functools.partial(merge_kernel, per, cq),
        out_shape=(jax.ShapeDtypeStruct((blocks, channels, cells), BF16), block_shape, block_shape),
        in_specs=[VMEM()] * (1 + tiles),
        out_specs=(VMEM(), VMEM(), VMEM()),
        compiler_params=params(),
        name="merge",
    )(order, arrived[0], *[arrived[hop] for hop in hop_order(tiles)])

    second = swapped(False, second, "tile")
    first = swapped(True, first, "tile")
    seam = shifted(coarse, "sect", 1)
    total, tables = pl.pallas_call(
        inside_kernel,
        out_shape=(
            jax.ShapeDtypeStruct(coarse.shape, F32),
            jax.ShapeDtypeStruct((2 + blocks,) + coarse_spatial.shape[1:], BF16),
        ),
        in_specs=[SMEM()] + [VMEM()] * 3,
        out_specs=(VMEM(), VMEM()),
        compiler_params=params(),
        name="inside",
    )(coarse_codes.transpose(1, 0, 2), coarse, coarse_spatial, coarse_mix)
    coarse_out = pl.pallas_call(
        coarse_kernel,
        out_shape=jax.ShapeDtypeStruct(coarse.shape, BF16),
        in_specs=[VMEM()] * 7,
        out_specs=VMEM(),
        compiler_params=params(),
        name="coarse",
    )(second, seam, first, coarse, total, tables, coarse_mix)
    return (skip[None, None], coarse_out[None, None])


def solution(mesh):
    data = P(("groups", "chan"), "sect", "tile", None, None)
    placed = (
        data,
        P(),
        P(),
        P("sect", "tile", None),
        P("sect", "tile", None),
        P(),
        P("sect", "tile"),
        P("sect", None),
        P(),
        P(),
        P("sect", "tile", None),
    )
    return jax.shard_map(
        per_device, mesh=mesh, in_specs=placed, out_specs=(data, data), check_vma=False
    )
```
